256 devices in a mesh: surf: 64 (over x, z, core), col: 4 (over y).
Axes of the slice: x: 4, y: 4, z: 8, core: 2. Of those that a mesh axis runs over, the one named last changes fastest.
Arguments:
- stiffness: float32 [256, 3, 512, 512], P(('surf', 'col'))
- load: float32 [256, 3, 512, 256], P(('surf', 'col')), may hold values from -6 to 6
- start: float32 [256, 3, 512, 256], P(('surf', 'col')), may hold values from -6 to 6
- boundary_matrix: float32 [4096, 4, 16384], P('surf', None, 'col'), may hold values from -0.046875 to 0.046875
- bem_node: int32 [4, 4096], P('col'), may hold values from 0 to 4095, as said below
Outputs:
- solution_field: float32 [256, 3, 512, 256], P(('surf', 'col'))
- traction: float32 [4, 4096, 256], P('col', 'surf')
The draws below stay inside these ranges and needn't reach their ends.
Inputs may be any that keep to these rules, and one draw needn't show every extreme that they name: Each row bem_node[g] is a permutation of 0 to 4096 - 1 (the top face nodes of column group g). For each block of 64 slots q in [s * 64, (s + 1) * 64) and each patch s2 of the group, the block's slots name either exactly 1 node of patch s2 or none; each patch's top face nodes lie in exactly 64 blocks.
All inputs are finite; a program needn't handle non-finite values.
Results may differ from the reference program's by a relative error of at most 0.0001.
Values sent between devices are 32-bit elements; how exact they have to be, the bound alone decides.
A program may use at most 128 MiB of HBM per device.

```python
import jax
import jax.numpy as jnp
from jax import lax

EDGE = 8
DEPTH = 3
FIELDS = 256
ITERS = 2
EL_NODES = 512
N_PATCH = 256
CB = 4096
NB = 16384
N_SURF = 64
N_COL = 4


def draw_stiffness(key, part):
    first = jax.random.fold_in(key, 0)
    shape = (N_PATCH, DEPTH, EL_NODES, EL_NODES)
    identity = jnp.eye(EL_NODES, dtype=jnp.float32)
    offdiag = jax.random.normal(first, shape, jnp.float32) * (0.6 / EL_NODES ** 0.5)
    return offdiag + 2.0 * identity


def draw_bem_node(key, part):
    face_nodes = EDGE * EDGE
    per_pair = max(face_nodes // N_SURF, 1)
    reach = min(N_SURF, face_nodes)

    def one_group(group_key):
        key_a, key_b, key_c, key_d = jax.random.split(group_key, 4)
        labels = jax.random.permutation(key_a, N_SURF)
        offsets = jax.random.permutation(key_b, N_SURF)
        slot_perm = jax.vmap(lambda small: jax.random.permutation(small, face_nodes))(jax.random.split(key_c, N_SURF))
        node_perm = jax.vmap(lambda small: jax.random.permutation(small, face_nodes))(jax.random.split(key_d, N_SURF))
        holder = jnp.arange(N_SURF, dtype=jnp.int32)[:, None]
        remain = slot_perm % reach
        within = slot_perm // reach
        owner = labels[(offsets[holder] + remain) % N_SURF]
        local_rank = remain * per_pair + within
        node_local = node_perm[owner, local_rank]
        return (owner * face_nodes + node_local).reshape(-1).astype(jnp.int32)
    return jax.vmap(one_group)(jax.random.split(key, N_COL))


def block_scale(rng, extent, shards, low, high):
    loudness, own = 1.0, jax.random.fold_in(rng, 6)
    for dim, blocks in shards:
        heights = jnp.exp(jax.random.uniform(jax.random.fold_in(own, dim), (blocks,), jnp.float32, low / len(shards), high / len(shards)))
        loudness = loudness * jnp.repeat(heights, extent[dim] // blocks).reshape([-1 if axis == dim else 1 for axis in range(len(extent))])
    return loudness


def scatter_about(rng, extent, deviation, bound, pieces=(), kind=jnp.bfloat16):
    gain = block_scale(rng, extent, pieces, -0.22, 0.18) if pieces else 1.0
    array = jax.random.normal(rng, extent, jnp.float32) * deviation * gain
    return jnp.minimum(jnp.maximum(array, -bound), bound).astype(kind)


def setup_inputs(seed: int = 0) -> dict:
    key_of = jax.random.split(jax.random.key(seed), 6)
    stiffness = draw_stiffness(jax.random.fold_in(key_of[5], 71), 0)
    load = scatter_about(key_of[1], (N_PATCH, DEPTH, EL_NODES, FIELDS), 1.0, 6.0, ((0, 256),), jnp.float32)
    start = scatter_about(key_of[2], (N_PATCH, DEPTH, EL_NODES, FIELDS), 1.0, 6.0, ((0, 256),), jnp.float32)
    boundary_matrix = scatter_about(key_of[3], (CB, N_COL, NB), NB ** -0.5, 0.046875, ((0, 64), (2, 4)), jnp.float32)
    bem_node = draw_bem_node(jax.random.fold_in(key_of[5], 71), 0)
    return dict(stiffness=stiffness, load=load, start=start, boundary_matrix=boundary_matrix, bem_node=bem_node)


damping = 0.25
coupling = 0.5


def face_terms(cube):
    low_i = cube[:, :, :, 0]
    high_i = cube[:, :, :, -1]
    below = jnp.concatenate([jnp.zeros_like(high_i[:1]), high_i[:-1]], axis=0)
    above = jnp.concatenate([low_i[1:], jnp.zeros_like(low_i[:1])], axis=0)
    extra = jnp.zeros_like(cube)
    extra = extra.at[:, :, :, 0].add(low_i - below)
    extra = extra.at[:, :, :, -1].add(high_i - above)
    low_j = cube[:, :, :, :, 0]
    high_j = cube[:, :, :, :, -1]
    left_side = jnp.concatenate([jnp.zeros_like(high_j[:, :1]), high_j[:, :-1]], axis=1)
    right_side = jnp.concatenate([low_j[:, 1:], jnp.zeros_like(low_j[:, :1])], axis=1)
    extra = extra.at[:, :, :, :, 0].add(low_j - left_side)
    extra = extra.at[:, :, :, :, -1].add(high_j - right_side)
    low_k = cube[:, :, :, :, :, 0]
    high_k = cube[:, :, :, :, :, -1]
    deeper = jnp.concatenate([low_k[:, :, 1:], jnp.zeros_like(low_k[:, :, :1])], axis=2)
    extra = extra.at[:, :, :, :, :, -1].add(high_k - deeper)
    extra = extra.at[:, :, 1:, :, :, 0].add(low_k[:, :, 1:] - high_k[:, :, :-1])
    return extra


def reference(stiffness, load, start, boundary_matrix, bem_node):
    highest = lax.Precision.HIGHEST
    shape_seven = (N_SURF, N_COL, DEPTH, EDGE, EDGE, EDGE, FIELDS)
    shape_five = (N_SURF, N_COL, DEPTH, EL_NODES, FIELDS)
    stiff_five = stiffness.reshape(N_SURF, N_COL, DEPTH, EL_NODES, EL_NODES)
    load_seven = load.reshape(shape_seven)
    current = start.reshape(shape_five)
    inverse = jnp.argsort(bem_node, axis=1).astype(jnp.int32)
    operator_rows = boundary_matrix.reshape(CB * N_COL, NB)
    traction = jnp.zeros((N_COL, CB, FIELDS), jnp.float32)
    for turn_index in range(ITERS):
        cube = current.reshape(shape_seven)
        top_face = cube[:, :, 0, :, :, 0, :]
        by_group = jnp.transpose(top_face, (1, 0, 2, 3, 4)).reshape(N_COL, CB, FIELDS)
        trace = jnp.take_along_axis(by_group, bem_node[:, :, None], axis=1)
        flat = jnp.dot(operator_rows, trace.reshape(NB, FIELDS), precision=highest,
                       preferred_element_type=jnp.float32)
        traction = jnp.transpose(flat.reshape(CB, N_COL, FIELDS), (1, 0, 2))
        on_nodes = jnp.take_along_axis(traction, inverse[:, :, None], axis=1)
        on_nodes = jnp.transpose(on_nodes.reshape(N_COL, N_SURF, EDGE, EDGE, FIELDS), (1, 0, 2, 3, 4))
        applied = jnp.einsum('scdab,scdbf->scdaf', stiff_five, current, precision=highest)
        applied = applied.reshape(shape_seven) + coupling * face_terms(cube)
        applied = applied.at[:, :, 0, :, :, 0, :].add(on_nodes)
        residual = load_seven - applied
        current = (cube + damping * residual).reshape(shape_five)
    return current.reshape(N_PATCH, DEPTH, EL_NODES, FIELDS), traction
```

```python
import functools

import jax
import jax.numpy as jnp
from jax import lax
from jax.experimental import pallas as pl
from jax.experimental.pallas import tpu as pltpu
from jax.sharding import PartitionSpec as P

MESH = pl.DeviceIdType.MESH
F32, BF16 = jnp.float32, jnp.bfloat16
NX, NZ, NC = 4, 8, 2
EDGE, DEPTH, NODES, FACE, FIELDS = 8, 3, 512, 64, 256
GROUPS, COLS = 4, 4096
SPLIT = 24
PARTS = (pl.ds(0, SPLIT), pl.ds(SPLIT, FACE - SPLIT))
damping = 0.25
coupling = 0.5


def sign(a):
    return 1 if a > 0 else -1


def halves(a):
    high = a.astype(BF16)
    return high, (a - high.astype(F32)).astype(BF16)


def dot(a, b):
    return jnp.dot(a, b, preferred_element_type=F32)


def dot3(ah, al, bh, bl):
    return dot(ah, bh) + dot(al, bh) + dot(ah, bl)


def exact(onehot, rows):
    return jnp.dot(onehot, rows, precision=lax.Precision.HIGHEST, preferred_element_type=F32)


def kernel(
    stiff, load, start, bm, map_a, map_b, sol, trac,
    u, v, ld, uh, ul, kraw, kh, kl, mraw, mh, ml, xb, part, rsbuf, halo, tr,
    asrc, abuf, bsrc, bbuf,
    lsem, gsend, grecv, asend, arecv, rsend, rrecv, hsend, hrecv, osem,
):
    s, y = lax.axis_index("surf"), lax.axis_index("col")
    c, z, x = s % NC, (s // NC) % NZ, s // (NC * NZ)
    sgn = 1 - 2 * c
    xc = x * NC + c
    u2, v2 = u.reshape(DEPTH, NODES, FIELDS), v.reshape(DEPTH, NODES, FIELDS)

    def at(dx, dz):
        return ((x + NX + dx) % NX * NZ + (z + NZ + dz) % NZ) * NC + c

    def chip(dx, dz):
        return (x + NX + dx) % NX * NZ + (z + NZ + dz) % NZ

    sibling = s + sgn
    up, down = (s + 1) % (NX * NZ * NC), (s + NX * NZ * NC - 1) % (NX * NZ * NC)

    def mate_xc(i):
        other = (xc + i) % (NX * NC)
        return other, (other // NC * NZ + z) * NC + other % NC

    def mate_z(i):
        other = (z + i) % NZ
        return other, (x * NZ + other) * NC + c

    lead = pltpu.make_async_copy(start.at[0], u2.at[0], lsem.at[0])
    rest = pltpu.make_async_copy(start.at[pl.ds(1, 2)], u2.at[pl.ds(1, 2)], lsem.at[1])
    get_m = pltpu.make_async_copy(bm, mraw, lsem.at[2])
    get_k = pltpu.make_async_copy(stiff, kraw, lsem.at[3])
    get_l = pltpu.make_async_copy(load, ld, lsem.at[4])
    for copy in (lead, rest, get_m, get_k, get_l):
        copy.start()

    barrier = pltpu.get_barrier_semaphore()

    def greet(surf, col):
        pl.semaphore_signal(barrier, inc=1, device_id=(surf, col), device_id_type=MESH)

    for i in range(1, NX * NC):
        greet(mate_xc(i)[1], y)
    for i in range(1, NZ):
        greet(mate_z(i)[1], y)
    for i in range(1, GROUPS):
        greet(s, (y + i) % GROUPS)
    greet((s + NX * NZ * NC - sgn) % (NX * NZ * NC), y)
    pl.semaphore_wait(barrier, NX * NC - 1 + NZ - 1 + GROUPS - 1 + 1)

    sub = lax.broadcasted_iota(jnp.int32, (FACE, FACE), 0)
    lane = lax.broadcasted_iota(jnp.int32, (FACE, FACE), 1)
    ma, mb = map_a[...], map_b[...]
    mine_a = jnp.sum(jnp.where((ma >> 6) == s, ma & 63, 0), axis=1, keepdims=True)
    lane_8 = lax.broadcasted_iota(jnp.int32, (FACE, NODES), 1)
    node_out = (mine_a * EDGE == lane_8).astype(F32)
    mine_b = jnp.sum(jnp.where((mb >> 6) == s, mb & 63, 0), axis=0, keepdims=True)
    sub_8 = lax.broadcasted_iota(jnp.int32, (NODES, FACE), 0)
    node_in = (mine_b * EDGE == sub_8).astype(F32)
    row = jnp.sum(jnp.where(sub == xc * NZ + z, ma, 0), axis=0, keepdims=True) >> 6
    slot_out = (((row >> 4) * NC + (row & 1)) * NZ + ((row >> 1) & 7) == sub).astype(F32)
    column = jnp.sum(jnp.where(lane == z * (NX * NC) + xc, mb, 0), axis=1, keepdims=True) >> 6
    slot_in = (((column >> 1) & 7) * (NX * NC) + (column >> 4) * NC + (column & 1) == lane).astype(F32)

    def eight(i):
        return pl.ds(pl.multiple_of(i * 8, 8), 8)

    def rows_out(k, rows):
        for h in range(2):
            asrc[k, h] = rows[:, 128 * h : 128 * h + 128]
        abuf[k, :, eight(xc)] = asrc[k, :, eight(xc)]
        for i in range(1, NX * NC):
            other, target = mate_xc(i)
            pltpu.make_async_remote_copy(
                src_ref=asrc.at[k, :, eight(other)], dst_ref=abuf.at[k, :, eight(xc)],
                send_sem=asend.at[k, 0], recv_sem=arecv.at[k, 0],
                device_id=(target, y), device_id_type=MESH,
            ).start()

    def rows_turn(k):
        seven = abuf.at[k, :, pl.ds(0, 56)]
        pltpu.make_async_copy(seven, seven, arecv.at[k, 0]).wait()
        for h in range(2):
            for i in range(NZ):
                bsrc[k, h, pl.ds(8 * i, 8)] = abuf[k, h, pl.ds(i, 8, stride=8)]
        bbuf[k, :, eight(z)] = bsrc[k, :, eight(z)]
        for i in range(1, NZ):
            other, target = mate_z(i)
            pltpu.make_async_remote_copy(
                src_ref=bsrc.at[k, :, eight(other)], dst_ref=bbuf.at[k, :, eight(z)],
                send_sem=asend.at[k, 1], recv_sem=arecv.at[k, 1],
                device_id=(target, y), device_id_type=MESH,
            ).start()

    def rows_in(k):
        seven = bbuf.at[k, :, pl.ds(0, 56)]
        pltpu.make_async_copy(seven, seven, arecv.at[k, 1]).wait()
        return jnp.concatenate([bbuf[k, 0], bbuf[k, 1]], axis=1)

    def split_m(p):
        def go():
            for g in range(GROUPS):
                for q in range(2):
                    tile = mraw[:, g, pl.ds(256 * p + 128 * q, 128)]
                    mh[2 * p + q, pl.ds(FACE * g, FACE)], ml[2 * p + q, pl.ds(FACE * g, FACE)] = halves(tile)
        return go

    def split_k(d, r):
        def go():
            kh[d, pl.ds(128 * r, 128)], kl[d, pl.ds(128 * r, 128)] = halves(kraw[d, pl.ds(128 * r, 128)])
        return go

    def split_u(w2, d):
        def go():
            uh[d], ul[d] = halves(w2[d])
        return go

    def face_out(it, w):
        def go():
            for k, (src, target) in enumerate((
                (w.at[:, 7], (up, y)),
                (w.at[:, 0], (down, y)),
                (w.at[:, :, 7], (s, (y + 1) % GROUPS)),
                (w.at[:, :, 0], (s, (y + GROUPS - 1) % GROUPS)),
            )):
                pltpu.make_async_remote_copy(
                    src_ref=src, dst_ref=halo.at[it, k], send_sem=hsend.at[it], recv_sem=hrecv.at[it],
                    device_id=target, device_id_type=MESH,
                ).start()
        return go

    def face_in(it):
        def go():
            pltpu.make_async_copy(halo.at[it], halo.at[it], hrecv.at[it]).wait()
        return go

    low_i = jnp.where(s > 0, 1.0, 0.0).astype(F32)
    high_i = jnp.where(s < NX * NZ * NC - 1, 1.0, 0.0).astype(F32)
    low_j = jnp.where(y > 0, 1.0, 0.0).astype(F32)
    high_j = jnp.where(y < GROUPS - 1, 1.0, 0.0).astype(F32)
    weight = damping * coupling

    layer = lax.broadcasted_iota(jnp.int32, (32, EDGE, FIELDS), 1)

    def volume(w2, o2, d, r):
        def go():
            block = pl.ds(256 * r, 256)
            applied = dot3(kh[d, block], kl[d, block], uh[d], ul[d])
            here = w2[d, block].reshape(32, EDGE, FIELDS)
            term = here
            if d + 1 < DEPTH:
                term = here - pltpu.roll(w2[d + 1, block].reshape(32, EDGE, FIELDS), 7, 1)
            term = jnp.where(layer == EDGE - 1, term, 0.0)
            if d:
                above = here - pltpu.roll(w2[d - 1, block].reshape(32, EDGE, FIELDS), 1, 1)
                term = jnp.where(layer == 0, above, term)
            out = w2[d, block] + damping * (ld[d, block] - applied)
            o2[d, block] = out - weight * term.reshape(256, FIELDS)
        return go

    def faces(it, w, o, w2, o2, d):
        def go():
            o[d, 0] -= weight * (w[d, 0] - low_i * halo[it, 0, d])
            o[d, 7] -= weight * (w[d, 7] - high_i * halo[it, 1, d])
            o[d, :, 0] -= weight * (w[d, :, 0] - low_j * halo[it, 2, d])
            o[d, :, 7] -= weight * (w[d, :, 7] - high_j * halo[it, 3, d])
        return go

    def boundary(it, spots):
        def go():
            left_h, left_l, right = [], [], []
            for dx, dz in spots:
                n = chip(-dx, -dz)
                left_h.append(mh[n])
                left_l.append(ml[n])
                right.append(xb[it, 2 * n])
                right.append(xb[it, 2 * n + 1])
            xh, xl = halves(jnp.concatenate(right, axis=0))
            part[...] += dot3(jnp.concatenate(left_h, axis=1), jnp.concatenate(left_l, axis=1), xh, xl)
        return go

    spots_of = [[] for _ in range(7)]
    for dx in (0, 1, -1, 2):
        for dz in (0, 1, -1, 2, -2, 3, -3, 4):
            spots_of[abs(dx) + abs(dz)].append((dx, dz))

    def gather(it, tasks, pops):
        tasks = list(tasks)
        xr = xb.at[it]

        def send(p, block, target):
            pltpu.make_async_remote_copy(
                src_ref=xr.at[block, PARTS[p]], dst_ref=xr.at[block, PARTS[p]],
                send_sem=gsend.at[it], recv_sem=grecv.at[it, p, block],
                device_id=(target, y), device_id_type=MESH,
            ).start()

        def wait(p, block):
            piece = xr.at[block, PARTS[p]]
            pltpu.make_async_copy(piece, piece, grecv.at[it, p, block]).wait()

        def share(block):
            pltpu.make_async_remote_copy(
                src_ref=xr.at[block], dst_ref=xr.at[block],
                send_sem=gsend.at[it], recv_sem=grecv.at[it, 0, block],
                device_id=(sibling, y), device_id_type=MESH,
            ).start()

        def shared(spots):
            def go():
                for dx, dz in spots:
                    block = at(-dx, -dz) + sgn
                    pltpu.make_async_copy(xr.at[block], xr.at[block], grecv.at[it, 0, block]).wait()
            return go

        def work(n):
            for _ in range(n):
                if tasks:
                    tasks.pop(0)()

        for p in (0, 1):
            for dx, dz in ((0, 1), (0, -1), (1, 0), (-1, 0)):
                send(p, s, at(dx, dz))
        share(s)
        part[...] = jnp.zeros_like(part)
        ready = list(spots_of[0])
        work(pops)
        for r in range(1, 7):
            for dx, dz in spots_of[r]:
                block = at(-dx, -dz)
                wait(0, block)
                if dz == 0:
                    send(0, block, at(0, 1))
                    send(0, block, at(0, -1))
                elif abs(dz) < 3 or (abs(dz) == 3 and (dx in (0, 1)) == (dz > 0)):
                    send(0, block, at(0, sign(dz)))
                wait(1, block)
                if dx == 0:
                    if abs(dz) < 3:
                        send(1, block, at(0, sign(dz)))
                    send(1, block, at(1, 0))
                    send(1, block, at(-1, 0))
                elif abs(dx) == 1 and (dz in (0, 1, -2, 3)) == (dx > 0):
                    send(1, block, at(sign(dx), 0))
                share(block)
                if (dx, dz) == (-1, 0):
                    send(0, at(-sgn, 0), at(sgn, 0))
                if (dx, dz) == (0, -3):
                    send(1, at(0, -3 * sgn), at(0, sgn))
                work(pops)
            ready += spots_of[r - 1] if r > 1 else []
            fresh = spots_of[r - 1]
            tasks.append(shared(fresh))
            while len(ready) >= 2:
                tasks.append(boundary(it, ready[:2]))
                ready = ready[2:]
        ready += spots_of[6]
        work(len(tasks))
        shared(spots_of[6])()
        boundary(it, ready)()

    def reduce(it):
        for i in range(1, GROUPS):
            other = (y + i) % GROUPS
            pltpu.make_async_remote_copy(
                src_ref=part.at[pl.ds(pl.multiple_of(FACE * other, FACE), FACE)], dst_ref=rsbuf.at[it, i - 1],
                send_sem=rsend.at[it], recv_sem=rrecv.at[it],
                device_id=(s, other), device_id_type=MESH,
            ).start()
        own = part[pl.ds(pl.multiple_of(FACE * y, FACE), FACE)]
        pltpu.make_async_copy(rsbuf.at[it], rsbuf.at[it], rrecv.at[it]).wait()
        total = own + rsbuf[it, 0] + rsbuf[it, 1] + rsbuf[it, 2]
        three = part.at[pl.ds(0, 3 * FACE)]
        pltpu.make_async_copy(three, three, rsend.at[it]).wait()
        return total

    lead.wait()
    rows_out(0, exact(node_out, u2[0]))
    rest.wait()
    rows_turn(0)
    xb[0, s] = exact(slot_in, rows_in(0))

    tasks = [get_m.wait] + [split_m(p) for p in range(16)]
    tasks += [face_out(0, u), get_k.wait] + [split_u(u2, d) for d in range(3)]
    tasks += [split_k(0, r) for r in range(4)] + [get_l.wait]
    tasks += [volume(u2, v2, 0, r) for r in range(2)]
    tasks += [face_in(0), faces(0, u, v, u2, v2, 0)]
    tasks += [lambda: rows_out(1, exact(node_out, v2[0]))]
    for d in (1, 2):
        tasks += [split_k(d, r) for r in range(4)] + [volume(u2, v2, d, r) for r in range(2)]
        tasks += [faces(0, u, v, u2, v2, d)]
    tasks += [lambda: rows_turn(1)]
    gather(0, tasks, 2)
    traction = reduce(0)
    xb[1, s] = exact(slot_in, rows_in(1)) - damping * traction
    tr[...] = traction

    def first_top():
        on_nodes = exact(node_in, rows_in(2))
        v2[0] -= damping * on_nodes
        pltpu.make_async_copy(halo.at[0], halo.at[0], hsend.at[0]).wait()

    tasks = [lambda: rows_out(2, exact(slot_out, tr[...])), lambda: None, lambda: rows_turn(2), lambda: None]
    tasks += [first_top, face_out(1, v)] + [split_u(v2, d) for d in range(3)]
    for d in (2, 1, 0):
        tasks += [volume(v2, u2, d, r) for r in range(2)]
    tasks += [face_in(1)] + [faces(1, v, u, v2, u2, d) for d in (2, 1, 0)]
    deep = pltpu.make_async_copy(u2.at[pl.ds(1, 2)], sol.at[pl.ds(1, 2)], osem.at[0])
    tasks += [deep.start]
    gather(1, tasks, 2)
    traction = reduce(1)
    tr[...] = traction
    rows_out(3, exact(slot_out, traction))
    put_tr = pltpu.make_async_copy(tr, trac, osem.at[1])
    put_tr.start()
    rows_turn(3)
    u2[0] -= damping * exact(node_in, rows_in(3))
    last = pltpu.make_async_copy(u2.at[0], sol.at[0], osem.at[2])
    last.start()

    for it in range(2):
        most = xb.at[it, pl.ds(0, 63)]
        pltpu.make_async_copy(most, most, gsend.at[it]).wait()
    pltpu.make_async_copy(halo.at[1], halo.at[1], hsend.at[1]).wait()
    for k in range(4):
        for phase in range(2):
            seven = abuf.at[k, :, pl.ds(0, 56)]
            pltpu.make_async_copy(seven, seven, asend.at[k, phase]).wait()
    deep.wait()
    put_tr.wait()
    last.wait()


def shards(stiffness, load, start, boundary_matrix, bem_node):
    nodes = bem_node.reshape(NX, NZ, NC, FACE)
    map_a = nodes.transpose(0, 2, 1, 3).reshape(FACE, FACE)
    map_b = nodes.transpose(3, 1, 0, 2).reshape(FACE, FACE)
    anywhere = pl.BlockSpec(memory_space=pl.ANY)
    vmem = pl.BlockSpec(memory_space=pltpu.VMEM)
    dma = pltpu.SemaphoreType.DMA
    field = (DEPTH, EDGE, EDGE, EDGE, FIELDS)
    flat = (DEPTH, NODES, FIELDS)
    sol, trac = pl.pallas_call(
        kernel,
        out_shape=(
            jax.ShapeDtypeStruct(flat, F32),
            jax.ShapeDtypeStruct((FACE, FIELDS), F32),
        ),
        in_specs=[anywhere] * 4 + [vmem] * 2,
        out_specs=(anywhere, anywhere),
        scratch_shapes=[
            pltpu.VMEM(field, F32), pltpu.VMEM(field, F32), pltpu.VMEM(flat, F32),
            pltpu.VMEM(flat, BF16), pltpu.VMEM(flat, BF16),
            pltpu.VMEM((DEPTH, NODES, NODES), F32),
            pltpu.VMEM((DEPTH, NODES, NODES), BF16), pltpu.VMEM((DEPTH, NODES, NODES), BF16),
            pltpu.VMEM((FACE, GROUPS, COLS), F32),
            pltpu.VMEM((32, 256, 128), BF16), pltpu.VMEM((32, 256, 128), BF16),
            pltpu.VMEM((2, 64, FACE, FIELDS), F32),
            pltpu.VMEM((256, FIELDS), F32),
            pltpu.VMEM((2, 3, FACE, FIELDS), F32),
            pltpu.VMEM((2, 4, DEPTH, EDGE, EDGE, FIELDS), F32),
            pltpu.VMEM((FACE, FIELDS), F32),
            *[pltpu.VMEM((4, 2, FACE, 128), F32)] * 4,
            dma((5,)), dma((2,)), dma((2, 2, 64)), dma((4, 2)), dma((4, 2)),
            dma((2,)), dma((2,)), dma((2,)), dma((2,)), dma((3,)),
        ],
        compiler_params=pltpu.CompilerParams(
            collective_id=0, has_side_effects=True, vmem_limit_bytes=58 * 2**20
        ),
        name="interface_iterations",
    )(stiffness[0], load[0], start[0], boundary_matrix, map_a, map_b)
    return sol[None], trac[None]


def solution(mesh):
    in_specs = (
        P(("surf", "col"), None, None, None),
        P(("surf", "col"), None, None, None),
        P(("surf", "col"), None, None, None),
        P("surf", None, "col"),
        P("col", None),
    )
    out_specs = (P(("surf", "col"), None, None, None), P("col", "surf", None))
    return jax.shard_map(shards, mesh=mesh, in_specs=in_specs, out_specs=out_specs, check_vma=False)
```

```python
import functools

import jax
import jax.numpy as jnp
from jax import lax
from jax.experimental import pallas as pl
from jax.experimental.pallas import tpu as pltpu
from jax.sharding import PartitionSpec as P

MESH = pl.DeviceIdType.MESH
F32, BF16 = jnp.float32, jnp.bfloat16
LAG = 8
NX, NZ, NC = 4, 8, 2
EDGE, DEPTH, NODES, FACE, FIELDS = 8, 3, 512, 64, 256
GROUPS, COLS = 4, 4096
SPLIT = 24
PARTS = (pl.ds(0, SPLIT), pl.ds(SPLIT, FACE - SPLIT))
damping = 0.25
coupling = 0.5


FIRST = (
    (0, 0, 1), (1, 0, -2), (1, 0, -1), (1, 0, 2), (0, 1, 0), (1, 0, 1), (0, 0, -2), (1, -1, 0), (0, -1, 0), (1, 1, 0),
)
ARRIVALS = (
    (0, 1, 0, ((0, -1), (1, 0))), (0, 0, 1, ((0, 2), (1, 0), (-1, 0))),
    (1, -1, 0, ((0, 1), (-1, 0))), (1, 1, 0, ()),
    (0, -1, 0, ()), (1, 0, -2, ((0, -1), (0, -2), (1, 0))),
    (1, 0, 2, ((-1, 0), (1, 0))), (1, 0, -1, ((-1, 0), (1, 0))),
    (1, 0, 1, ((1, 0),)), (0, 2, 0, ((0, 1),)),
    (0, -1, 1, ((0, 1),)), (0, 0, -2, ((0, -1), (1, 0), (0, 1), (-1, 0))),
    (0, 1, 1, ((0, 1),)), (0, 1, -1, ((1, 0),)),
    (0, 0, 3, ((-1, 0), (0, 1))), (1, 2, 0, ()),
    (1, 1, -2, ()), (1, 0, -3, ((-1, 0), (1, 0))),
    (1, -1, 1, ()), (1, -1, 2, ((-1, 0),)),
    (1, 1, 2, ((0, 1),)), (1, -1, -1, ((-1, 0),)),
    (1, 0, 4, ((0, -1), (1, 0))), (1, 1, -1, ()),
    (0, -1, -2, ()), (0, -1, 3, ((-1, 0), (0, 1))),
    (1, 1, 1, ((1, 0),)), (0, 2, 1, ()),
    (0, 1, -2, ((0, -1), (1, 0))), (0, -1, 2, ()),
    (1, -1, -3, ((0, 1), (0, -1), (-1, 0))), (0, 2, -1, ((1, 0), (0, -2))),
    (0, 0, -1, ()), (1, 2, 2, ((0, 1),)),
    (1, 1, -3, ()), (0, 1, 2, ((-1, 0), (0, 1), (1, 0))),
    (0, 0, -3, ((-1, 0),)), (0, 0, 4, ((1, 0),)),
    (1, 2, -1, ((0, -1),)), (1, 1, 4, ((1, 0),)),
    (1, 0, 3, ((-1, 0),)), (0, 2, 3, ((0, 1),)),
    (1, 1, 3, ()), (1, 2, 1, ()),
    (0, 1, -3, ()), (0, -1, 4, ()),
    (0, 2, -2, ()), (1, 2, -3, ()),
    (1, -1, 4, ()), (0, -1, -1, ()),
    (1, -1, -2, ()), (0, 0, 2, ()),
    (0, 2, 2, ()), (0, -1, -3, ()),
    (1, 2, 3, ()), (0, 2, -3, ()),
    (0, 1, 4, ()), (0, 1, 3, ()),
    (1, -1, 3, ()), (1, 2, -2, ()),
    (1, 2, 4, ()), (0, 2, 4, ()),
)


def halves(a):
    high = a.astype(BF16)
    return high, (a - high.astype(F32)).astype(BF16)


def dot(a, b):
    return jnp.dot(a, b, preferred_element_type=F32)


def dot_t(a, b):
    return lax.dot_general(a, b, (((1,), (1,)), ((), ())), preferred_element_type=F32)


def dot3(ah, al, bh, bl):
    return dot(ah, bh) + dot(al, bh) + dot(ah, bl)


def exact(onehot, rows):
    high, low = halves(rows)
    least = (rows - high.astype(F32) - low.astype(F32)).astype(BF16)
    return dot(onehot, high) + dot(onehot, low) + dot(onehot, least)


def kernel(
    stiff, load, start, bm, nodes, sol, trac,
    u, v, ld, uh, ul, kraw, kh, kl, mraw, mh, ml, nh, nl, xb, part, rsbuf, halo, tr,
    asrc, abuf, bsrc, bbuf,
    lsem, gsend, grecv, asend, arecv, rsend, rrecv, hsend, hrecv, osem,
):
    s, y = lax.axis_index("surf"), lax.axis_index("col")
    c, z, x = s % NC, (s // NC) % NZ, s // (NC * NZ)
    sgn = 1 - 2 * c
    xc = c * NX + x
    u2, v2 = u.reshape(DEPTH, NODES, FIELDS), v.reshape(DEPTH, NODES, FIELDS)

    def at(dx, dz):
        return ((x + NX + dx) % NX * NZ + (z + NZ + dz) % NZ) * NC + c

    def chip(dx, dz):
        return (x + NX + dx) % NX * NZ + (z + NZ + dz) % NZ

    sibling = s + sgn
    up, down = (s + 1) % (NX * NZ * NC), (s + NX * NZ * NC - 1) % (NX * NZ * NC)

    def mate_xc(i):
        other = (xc + i) % (NX * NC)
        return other, (other % NX * NZ + z) * NC + other // NX

    def mate_z(i):
        other = (z + i) % NZ
        return other, (x * NZ + other) * NC + c

    lead = pltpu.make_async_copy(start.at[0], u2.at[0], lsem.at[0])
    rest = pltpu.make_async_copy(start.at[pl.ds(1, 2)], u2.at[pl.ds(1, 2)], lsem.at[1])
    get_m = [pltpu.make_async_copy(bm.at[:, g], mraw.at[g], lsem.at[5 + g]) for g in range(GROUPS)]
    get_k = pltpu.make_async_copy(stiff, kraw, lsem.at[3])
    get_l = pltpu.make_async_copy(load, ld, lsem.at[4])
    for copy in (lead, *get_m, rest, get_k, get_l):
        copy.start()

    barrier = pltpu.get_barrier_semaphore()

    def greet(surf, col):
        pl.semaphore_signal(barrier, inc=1, device_id=(surf, col), device_id_type=MESH)

    for i in range(1, NX * NC):
        greet(mate_xc(i)[1], y)
    for i in range(1, NZ):
        greet(mate_z(i)[1], y)
    for i in range(1, GROUPS):
        greet(s, (y + i) % GROUPS)
    greet((s + NX * NZ * NC - sgn) % (NX * NZ * NC), y)
    pl.semaphore_wait(barrier, NX * NC - 1 + NZ - 1 + GROUPS - 1 + 1)

    sub = lax.broadcasted_iota(jnp.int32, (FACE, FACE), 0)
    lane = lax.broadcasted_iota(jnp.int32, (FACE, FACE), 1)
    pairs = nodes[...]
    held = jnp.concatenate([pairs[:, :FACE], pairs[:, FACE:]], axis=0)
    mine = jnp.sum(jnp.where((held >> 6) == s, held & 63, 0), axis=1, keepdims=True)
    lane_8 = lax.broadcasted_iota(jnp.int32, (FACE, NODES), 1)
    node_out = (mine * EDGE == lane_8).astype(F32).astype(BF16)
    turned = jnp.sum(jnp.where(sub == (lane & 7) * 8 + (lane >> 3), mine, 0), axis=0, keepdims=True)
    sub_8 = lax.broadcasted_iota(jnp.int32, (NODES, FACE), 0)
    node_in = (turned * EDGE == sub_8).astype(F32).astype(BF16)
    patch = jnp.sum(jnp.where(sub == xc * NZ + z, held, 0), axis=0, keepdims=True) >> 6
    slot_out = ((patch & 1) * 32 + (patch >> 1) == sub).astype(F32).astype(BF16)
    column = jnp.sum(jnp.where(sub == lane, patch, 0), axis=1, keepdims=True)
    slot_in = (((column >> 1) & 7) * 8 + (column & 1) * NX + (column >> 4) == lane).astype(F32).astype(BF16)

    def eight(i):
        return pl.ds(pl.multiple_of(i * 8, 8), 8)

    def rows_out(k, rows):
        for h in range(2):
            asrc[k, h] = rows[:, 128 * h : 128 * h + 128]
        abuf[k, :, eight(xc)] = asrc[k, :, eight(xc)]
        for i in range(1, NX * NC):
            other, target = mate_xc(i)
            pltpu.make_async_remote_copy(
                src_ref=asrc.at[k, :, eight(other)], dst_ref=abuf.at[k, :, eight(xc)],
                send_sem=asend.at[k, 0], recv_sem=arecv.at[k, 0],
                device_id=(target, y), device_id_type=MESH,
            ).start()

    def rows_turn(k):
        seven = abuf.at[k, :, pl.ds(0, 56)]
        pltpu.make_async_copy(seven, seven, arecv.at[k, 0]).wait()
        for h in range(2):
            for i in range(NZ):
                bsrc[k, h, pl.ds(8 * i, 8)] = abuf[k, h, pl.ds(i, 8, stride=8)]
        bbuf[k, :, eight(z)] = bsrc[k, :, eight(z)]
        for i in range(1, NZ):
            other, target = mate_z(i)
            pltpu.make_async_remote_copy(
                src_ref=bsrc.at[k, :, eight(other)], dst_ref=bbuf.at[k, :, eight(z)],
                send_sem=asend.at[k, 1], recv_sem=arecv.at[k, 1],
                device_id=(target, y), device_id_type=MESH,
            ).start()

    def rows_in(k):
        seven = bbuf.at[k, :, pl.ds(0, 56)]
        pltpu.make_async_copy(seven, seven, arecv.at[k, 1]).wait()
        return jnp.concatenate([bbuf[k, 0], bbuf[k, 1]], axis=1)

    big_sub = lax.broadcasted_iota(jnp.int32, (128, 128), 0)
    big_lane = lax.broadcasted_iota(jnp.int32, (128, 128), 1)

    def split_m(p):
        def go():
            for n in (2 * p, 2 * p + 1):
                for g in range(GROUPS):
                    tile = mraw[g, :, pl.ds(128 * n, 128)]
                    mh[n, pl.ds(FACE * g, FACE)], ml[n, pl.ds(FACE * g, FACE)] = halves(tile)
        return go

    named = dot_t((big_sub == big_lane).astype(F32).astype(BF16), (pairs >> 6).astype(F32).astype(BF16))
    wide_sub = lax.broadcasted_iota(jnp.int32, (256, 256), 0)
    wide_lane = lax.broadcasted_iota(jnp.int32, (256, 256), 1)
    wanted = jnp.where((wide_sub >> 6) == (wide_lane >> 6), wide_lane & 63, -1).astype(F32)

    def order_m(n):
        def go():
            row = jnp.concatenate([named[:, 2 * n : 2 * n + 1], named[:, 2 * n + 1 : 2 * n + 2]], axis=0)
            place = jnp.where(row == wanted, 1.0, 0.0).astype(BF16)
            nh[n] = dot(jnp.concatenate([mh[2 * n], mh[2 * n + 1]], axis=1), place).astype(BF16)
            nl[n] = dot(jnp.concatenate([ml[2 * n], ml[2 * n + 1]], axis=1), place).astype(BF16)
        return go

    def split_k(d, r):
        def go():
            kh[d, pl.ds(128 * r, 128)], kl[d, pl.ds(128 * r, 128)] = halves(kraw[d, pl.ds(128 * r, 128)])
        return go

    def split_u(w2, d):
        def go():
            uh[d], ul[d] = halves(w2[d])
        return go

    def face_out(it, w):
        def go():
            for k, (src, target) in enumerate((
                (w.at[:, 7], (up, y)),
                (w.at[:, 0], (down, y)),
                (w.at[:, :, 7], (s, (y + 1) % GROUPS)),
                (w.at[:, :, 0], (s, (y + GROUPS - 1) % GROUPS)),
            )):
                pltpu.make_async_remote_copy(
                    src_ref=src, dst_ref=halo.at[it, k], send_sem=hsend.at[it], recv_sem=hrecv.at[it],
                    device_id=target, device_id_type=MESH,
                ).start()
        return go

    def face_in(it):
        def go():
            pltpu.make_async_copy(halo.at[it], halo.at[it], hrecv.at[it]).wait()
        return go

    low_i = jnp.where(s > 0, 1.0, 0.0).astype(F32)
    high_i = jnp.where(s < NX * NZ * NC - 1, 1.0, 0.0).astype(F32)
    low_j = jnp.where(y > 0, 1.0, 0.0).astype(F32)
    high_j = jnp.where(y < GROUPS - 1, 1.0, 0.0).astype(F32)
    weight = damping * coupling

    layer = lax.broadcasted_iota(jnp.int32, (32, EDGE, FIELDS), 1)

    def volume(w2, o2, d, r):
        def go():
            block = pl.ds(256 * r, 256)
            applied = dot3(kh[d, block], kl[d, block], uh[d], ul[d])
            here = w2[d, block].reshape(32, EDGE, FIELDS)
            term = here
            if d + 1 < DEPTH:
                term = here - pltpu.roll(w2[d + 1, block].reshape(32, EDGE, FIELDS), 7, 1)
            term = jnp.where(layer == EDGE - 1, term, 0.0)
            if d:
                above = here - pltpu.roll(w2[d - 1, block].reshape(32, EDGE, FIELDS), 1, 1)
                term = jnp.where(layer == 0, above, term)
            out = w2[d, block] + damping * (ld[d, block] - applied)
            o2[d, block] = out - weight * term.reshape(256, FIELDS)
        return go

    def faces(it, w, o, w2, o2, d):
        def go():
            o[d, 0] -= weight * (w[d, 0] - low_i * halo[it, 0, d])
            o[d, 7] -= weight * (w[d, 7] - high_i * halo[it, 1, d])
            o[d, :, 0] -= weight * (w[d, :, 0] - low_j * halo[it, 2, d])
            o[d, :, 7] -= weight * (w[d, :, 7] - high_j * halo[it, 3, d])
        return go

    x2 = xb.reshape(2, 2, 64 * FACE, 128)

    def boundary(it, spots):
        def go():
            left_h, left_l, right = [], [], []
            for dx, dz in spots:
                n = chip(-dx, -dz)
                left_h.append(mh[n])
                left_l.append(ml[n])
                rows = pl.ds(pl.multiple_of(128 * n, 128), 128)
                right.append(jnp.concatenate([x2[it, 0, rows], x2[it, 1, rows]], axis=1))
            xh, xl = halves(jnp.concatenate(right, axis=0))
            part[...] += dot3(jnp.concatenate(left_h, axis=1), jnp.concatenate(left_l, axis=1), xh, xl)
        return go

    def boundary_by_node(n):
        right = []
        for block in range(2 * n, 2 * n + 4):
            rows = pl.ds(block % 2 * 32 + block // 2, FACE, stride=FACE)
            right.append(jnp.concatenate([x2[0, 0, rows], x2[0, 1, rows]], axis=1))
        xh, xl = halves(jnp.concatenate(right, axis=0))
        part[...] += dot3(nh[n // 2], nl[n // 2], xh, xl)

    def put_x(it, rows):
        for h in range(2):
            xb[it, h, s] = rows[:, 128 * h : 128 * h + 128]

    def gather(it, tasks, pops):
        tasks = list(tasks)
        xr = xb.at[it]

        def send(p, block, target):
            pltpu.make_async_remote_copy(
                src_ref=xr.at[:, block, PARTS[p]], dst_ref=xr.at[:, block, PARTS[p]],
                send_sem=gsend.at[it], recv_sem=grecv.at[it, p, block],
                device_id=(target, y), device_id_type=MESH,
            ).start()

        def wait(p, block):
            piece = xr.at[:, block, PARTS[p]]
            pltpu.make_async_copy(piece, piece, grecv.at[it, p, block]).wait()

        def share(block):
            pltpu.make_async_remote_copy(
                src_ref=xr.at[:, block], dst_ref=xr.at[:, block],
                send_sem=gsend.at[it], recv_sem=grecv.at[it, 0, block],
                device_id=(sibling, y), device_id_type=MESH,
            ).start()

        def shared(spots):
            def go():
                for dx, dz in spots:
                    block = at(-dx, -dz) + sgn
                    pltpu.make_async_copy(xr.at[:, block], xr.at[:, block], grecv.at[it, 0, block]).wait()
            return go

        def work(now, most):
            while tasks and tasks[0][0] <= now and most:
                tasks.pop(0)[1]()
                most -= 1

        for p, dx, dz in FIRST:
            send(p, s, at(dx, dz))
        share(s)
        part[...] = jnp.zeros_like(part)
        work(-1, pops)
        seen, fresh = {(0, 0): 2}, [(0, 0)]
        for now, (p, dx, dz, onward) in enumerate(ARRIVALS):
            block = at(-dx, -dz)
            wait(p, block)
            for tx, tz in onward:
                send(p, block, at(tx, tz))
            seen[dx, dz] = seen.get((dx, dz), 0) + 1
            if seen[dx, dz] == 2:
                share(block)
                fresh.append((dx, dz))
            if it and now >= 12 and len(fresh) > LAG:
                early, fresh = fresh[:2], fresh[2:]
                tasks[:0] = [(0, shared(early)), (0, boundary(it, early))]
            work(now, pops)
        work(99, 99)
        shared(fresh)()
        if it:
            for i in range(0, len(fresh), 4):
                boundary(it, fresh[i : i + 4])()
        else:
            for n in range(0, 32, 2):
                boundary_by_node(n)

    def reduce(it, tasks):
        for i in (2, 1, 3):
            other = (y + i) % GROUPS
            pltpu.make_async_remote_copy(
                src_ref=part.at[pl.ds(pl.multiple_of(FACE * other, FACE), FACE)], dst_ref=rsbuf.at[it, i - 1],
                send_sem=rsend.at[it], recv_sem=rrecv.at[it],
                device_id=(s, other), device_id_type=MESH,
            ).start()
        for task in tasks:
            task()
        own = part[pl.ds(pl.multiple_of(FACE * y, FACE), FACE)]
        pltpu.make_async_copy(rsbuf.at[it], rsbuf.at[it], rrecv.at[it]).wait()
        total = own + rsbuf[it, 0] + rsbuf[it, 1] + rsbuf[it, 2]
        three = part.at[pl.ds(0, 3 * FACE)]
        pltpu.make_async_copy(three, three, rsend.at[it]).wait()
        return total

    lead.wait()
    put_x(0, exact(node_out, u2[0]))
    early = [rest.wait] + [copy.wait for copy in get_m] + [split_m(p) for p in range(16)] + [order_m(n) for n in range(16)]
    later = [get_k.wait] + [split_u(u2, d) for d in range(3)]
    later += [split_k(0, r) for r in range(4)] + [get_l.wait] + [volume(u2, v2, 0, r) for r in range(2)]
    tasks = [(-1, task) for task in early[:13]] + [(0, task) for task in early[13:]]
    tasks[13:13] = [(3, face_out(0, u))]
    tasks += [(0, task) for task in later]
    tasks += [(36, face_in(0)), (36, faces(0, u, v, u2, v2, 0))]
    tasks += [(36, lambda: rows_out(1, exact(node_out, v2[0])))]
    for d in (1, 2):
        tasks += [(0, split_k(d, r)) for r in range(4)] + [(0, volume(u2, v2, d, r)) for r in range(2)]
        tasks += [(0, faces(0, u, v, u2, v2, d))]
    tasks += [(56, lambda: rows_turn(1))]
    gather(0, tasks, 3)
    traction = reduce(0, [])
    put_x(1, exact(slot_in, rows_in(1)) - damping * traction)
    tr[...] = traction

    def first_top():
        v2[0] -= damping * exact(node_in, rows_in(2))
        pltpu.make_async_copy(halo.at[0], halo.at[0], hsend.at[0]).wait()

    tasks = [(-1, lambda: rows_out(2, exact(slot_out, tr[...]))), (14, lambda: rows_turn(2))]
    tasks += [(30, first_top), (30, face_out(1, v))] + [(30, split_u(v2, d)) for d in range(3)]
    for d in (2, 1, 0):
        tasks += [(0, volume(v2, u2, d, r)) for r in range(2)]
    gather(1, tasks, 3)
    deep = pltpu.make_async_copy(u2.at[pl.ds(1, 2)], sol.at[pl.ds(1, 2)], osem.at[0])
    traction = reduce(1, [face_in(1)] + [faces(1, v, u, v2, u2, d) for d in (2, 1, 0)] + [deep.start])
    tr[...] = traction
    rows_out(3, exact(slot_out, traction))
    put_tr = pltpu.make_async_copy(tr, trac, osem.at[1])
    put_tr.start()
    rows_turn(3)
    u2[0] -= damping * exact(node_in, rows_in(3))
    last = pltpu.make_async_copy(u2.at[0], sol.at[0], osem.at[2])
    last.start()

    for it in range(2):
        most = xb.at[it, :, pl.ds(0, 63)]
        pltpu.make_async_copy(most, most, gsend.at[it]).wait()
    pltpu.make_async_copy(halo.at[1], halo.at[1], hsend.at[1]).wait()
    for k in (1, 2, 3):
        for phase in range(2):
            seven = abuf.at[k, :, pl.ds(0, 56)]
            pltpu.make_async_copy(seven, seven, asend.at[k, phase]).wait()
    deep.wait()
    put_tr.wait()
    last.wait()


def shards(stiffness, load, start, boundary_matrix, bem_node):
    anywhere = pl.BlockSpec(memory_space=pl.ANY)
    vmem = pl.BlockSpec(memory_space=pltpu.VMEM)
    dma = pltpu.SemaphoreType.DMA
    field = (DEPTH, EDGE, EDGE, EDGE, FIELDS)
    flat = (DEPTH, NODES, FIELDS)
    sol, trac = pl.pallas_call(
        kernel,
        out_shape=(
            jax.ShapeDtypeStruct(flat, F32),
            jax.ShapeDtypeStruct((FACE, FIELDS), F32),
        ),
        in_specs=[anywhere] * 4 + [vmem],
        out_specs=(anywhere, anywhere),
        scratch_shapes=[
            pltpu.VMEM(field, F32), pltpu.VMEM(field, F32), pltpu.VMEM(flat, F32),
            pltpu.VMEM(flat, BF16), pltpu.VMEM(flat, BF16),
            pltpu.VMEM((DEPTH, NODES, NODES), F32),
            pltpu.VMEM((DEPTH, NODES, NODES), BF16), pltpu.VMEM((DEPTH, NODES, NODES), BF16),
            pltpu.VMEM((GROUPS, FACE, COLS), F32),
            *[pltpu.VMEM((32, 256, 128), BF16)] * 2,
            *[pltpu.VMEM((16, 256, 256), BF16)] * 2,
            pltpu.VMEM((2, 2, 64, FACE, 128), F32),
            pltpu.VMEM((256, FIELDS), F32),
            pltpu.VMEM((2, 3, FACE, FIELDS), F32),
            pltpu.VMEM((2, 4, DEPTH, EDGE, EDGE, FIELDS), F32),
            pltpu.VMEM((FACE, FIELDS), F32),
            *[pltpu.VMEM((4, 2, FACE, 128), F32)] * 4,
            dma((9,)), dma((2,)), dma((2, 2, 64)), dma((4, 2)), dma((4, 2)),
            dma((2,)), dma((2,)), dma((2,)), dma((2,)), dma((3,)),
        ],
        compiler_params=pltpu.CompilerParams(
            collective_id=0, has_side_effects=True, vmem_limit_bytes=58 * 2**20
        ),
        name="interface_iterations",
    )(stiffness[0], load[0], start[0], boundary_matrix, bem_node.reshape(32, 128))
    return sol[None], trac[None]


def solution(mesh):
    in_specs = (
        P(("surf", "col"), None, None, None),
        P(("surf", "col"), None, None, None),
        P(("surf", "col"), None, None, None),
        P("surf", None, "col"),
        P("col", None),
    )
    out_specs = (P(("surf", "col"), None, None, None), P("col", "surf", None))
    return jax.shard_map(shards, mesh=mesh, in_specs=in_specs, out_specs=out_specs, check_vma=False)
```

```python
import functools

import jax
import jax.numpy as jnp
from jax import lax
from jax.experimental import pallas as pl
from jax.experimental.pallas import tpu as pltpu
from jax.sharding import PartitionSpec as P

MESH = pl.DeviceIdType.MESH
F32, BF16 = jnp.float32, jnp.bfloat16
START = (30, 12)
LAG = 8
NX, NZ, NC = 4, 8, 2
EDGE, DEPTH, NODES, FACE, FIELDS = 8, 3, 512, 64, 256
GROUPS, COLS = 4, 4096
SPLIT = 24
PARTS = (pl.ds(0, SPLIT), pl.ds(SPLIT, FACE - SPLIT))
damping = 0.25
coupling = 0.5


FIRST = (
    (0, 0, 1), (1, 0, -2), (1, 0, -1), (1, 0, 2), (0, 1, 0), (1, 0, 1), (0, 0, -2), (1, -1, 0), (0, -1, 0), (1, 1, 0),
)
ARRIVALS = (
    (0, 1, 0, ((0, -1), (1, 0))), (0, 0, 1, ((0, 2), (1, 0), (-1, 0))),
    (1, -1, 0, ((0, 1), (-1, 0))), (1, 1, 0, ()),
    (0, -1, 0, ()), (1, 0, -2, ((0, -1), (0, -2), (1, 0))),
    (1, 0, 2, ((-1, 0), (1, 0))), (1, 0, -1, ((-1, 0), (1, 0))),
    (1, 0, 1, ((1, 0),)), (0, 2, 0, ((0, 1),)),
    (0, -1, 1, ((0, 1),)), (0, 0, -2, ((0, -1), (1, 0), (0, 1), (-1, 0))),
    (0, 1, 1, ((0, 1),)), (0, 1, -1, ((1, 0),)),
    (0, 0, 3, ((-1, 0), (0, 1))), (1, 2, 0, ()),
    (1, 1, -2, ()), (1, 0, -3, ((-1, 0), (1, 0))),
    (1, -1, 1, ()), (1, -1, 2, ((-1, 0),)),
    (1, 1, 2, ((0, 1),)), (1, -1, -1, ((-1, 0),)),
    (1, 0, 4, ((0, -1), (1, 0))), (1, 1, -1, ()),
    (0, -1, -2, ()), (0, -1, 3, ((-1, 0), (0, 1))),
    (1, 1, 1, ((1, 0),)), (0, 2, 1, ()),
    (0, 1, -2, ((0, -1), (1, 0))), (0, -1, 2, ()),
    (1, -1, -3, ((0, 1), (0, -1), (-1, 0))), (0, 2, -1, ((1, 0), (0, -2))),
    (0, 0, -1, ()), (1, 2, 2, ((0, 1),)),
    (1, 1, -3, ()), (0, 1, 2, ((-1, 0), (0, 1), (1, 0))),
    (0, 0, -3, ((-1, 0),)), (0, 0, 4, ((1, 0),)),
    (1, 2, -1, ((0, -1),)), (1, 1, 4, ((1, 0),)),
    (1, 0, 3, ((-1, 0),)), (0, 2, 3, ((0, 1),)),
    (1, 1, 3, ()), (1, 2, 1, ()),
    (0, 1, -3, ()), (0, -1, 4, ()),
    (0, 2, -2, ()), (1, 2, -3, ()),
    (1, -1, 4, ()), (0, -1, -1, ()),
    (1, -1, -2, ()), (0, 0, 2, ()),
    (0, 2, 2, ()), (0, -1, -3, ()),
    (1, 2, 3, ()), (0, 2, -3, ()),
    (0, 1, 4, ()), (0, 1, 3, ()),
    (1, -1, 3, ()), (1, 2, -2, ()),
    (1, 2, 4, ()), (0, 2, 4, ()),
)


def halves(a):
    high = a.astype(BF16)
    return high, (a - high.astype(F32)).astype(BF16)


def dot(a, b):
    return jnp.dot(a, b, preferred_element_type=F32)


def dot_t(a, b):
    return lax.dot_general(a, b, (((1,), (1,)), ((), ())), preferred_element_type=F32)


def dot3(ah, al, bh, bl):
    return dot(ah, bh) + dot(al, bh) + dot(ah, bl)


def exact(onehot, rows):
    high, low = halves(rows)
    least = (rows - high.astype(F32) - low.astype(F32)).astype(BF16)
    return dot(onehot, high) + dot(onehot, low) + dot(onehot, least)


def kernel(
    stiff, load, start, bm, nodes, sol, trac,
    u, v, ld, uh, ul, kraw, kh, kl, mraw, mh, ml, nh, nl, turned_m, xb, part, rsbuf, halo, tr,
    asrc, abuf, bsrc, bbuf,
    lsem, gsend, grecv, asend, arecv, rsend, rrecv, hsend, hrecv, osem,
):
    s, y = lax.axis_index("surf"), lax.axis_index("col")
    c, z, x = s % NC, (s // NC) % NZ, s // (NC * NZ)
    sgn = 1 - 2 * c
    xc = c * NX + x
    u2, v2 = u.reshape(DEPTH, NODES, FIELDS), v.reshape(DEPTH, NODES, FIELDS)

    def at(dx, dz):
        return ((x + NX + dx) % NX * NZ + (z + NZ + dz) % NZ) * NC + c

    def chip(dx, dz):
        return (x + NX + dx) % NX * NZ + (z + NZ + dz) % NZ

    sibling = s + sgn
    up, down = (s + 1) % (NX * NZ * NC), (s + NX * NZ * NC - 1) % (NX * NZ * NC)

    def mate_xc(i):
        other = (xc + i) % (NX * NC)
        return other, (other % NX * NZ + z) * NC + other // NX

    def mate_z(i):
        other = (z + i) % NZ
        return other, (x * NZ + other) * NC + c

    lead = pltpu.make_async_copy(start.at[0], u2.at[0], lsem.at[0])
    rest = pltpu.make_async_copy(start.at[pl.ds(1, 2)], u2.at[pl.ds(1, 2)], lsem.at[1])
    get_m = [pltpu.make_async_copy(bm.at[:, g], mraw.at[g], lsem.at[5 + g]) for g in range(GROUPS)]
    get_k = pltpu.make_async_copy(stiff, kraw, lsem.at[3])
    get_l = pltpu.make_async_copy(load, ld, lsem.at[4])
    for copy in (lead, *get_m, rest, get_k, get_l):
        copy.start()

    barrier = pltpu.get_barrier_semaphore()

    def greet(surf, col):
        pl.semaphore_signal(barrier, inc=1, device_id=(surf, col), device_id_type=MESH)

    for i in range(1, NX * NC):
        greet(mate_xc(i)[1], y)
    for i in range(1, NZ):
        greet(mate_z(i)[1], y)
    for i in range(1, GROUPS):
        greet(s, (y + i) % GROUPS)
    greet((s + NX * NZ * NC - sgn) % (NX * NZ * NC), y)
    pl.semaphore_wait(barrier, NX * NC - 1 + NZ - 1 + GROUPS - 1 + 1)

    sub = lax.broadcasted_iota(jnp.int32, (FACE, FACE), 0)
    lane = lax.broadcasted_iota(jnp.int32, (FACE, FACE), 1)
    pairs = nodes[...]
    held = jnp.concatenate([pairs[:, :FACE], pairs[:, FACE:]], axis=0)
    mine = jnp.sum(jnp.where((held >> 6) == s, held & 63, 0), axis=1, keepdims=True)
    lane_8 = lax.broadcasted_iota(jnp.int32, (FACE, NODES), 1)
    node_out = (mine * EDGE == lane_8).astype(F32).astype(BF16)
    turned = jnp.sum(jnp.where(sub == (lane & 7) * 8 + (lane >> 3), mine, 0), axis=0, keepdims=True)
    sub_8 = lax.broadcasted_iota(jnp.int32, (NODES, FACE), 0)
    node_in = (turned * EDGE == sub_8).astype(F32).astype(BF16)
    patch = jnp.sum(jnp.where(sub == xc * NZ + z, held, 0), axis=0, keepdims=True) >> 6
    slot_out = ((patch & 1) * 32 + (patch >> 1) == sub).astype(F32).astype(BF16)
    column = jnp.sum(jnp.where(sub == lane, patch, 0), axis=1, keepdims=True)
    slot_in = (((column >> 1) & 7) * 8 + (column & 1) * NX + (column >> 4) == lane).astype(F32).astype(BF16)

    def eight(i):
        return pl.ds(pl.multiple_of(i * 8, 8), 8)

    def rows_out(k, rows):
        for h in range(2):
            asrc[k, h] = rows[:, 128 * h : 128 * h + 128]
        abuf[k, :, eight(xc)] = asrc[k, :, eight(xc)]
        for i in range(1, NX * NC):
            other, target = mate_xc(i)
            pltpu.make_async_remote_copy(
                src_ref=asrc.at[k, :, eight(other)], dst_ref=abuf.at[k, :, eight(xc)],
                send_sem=asend.at[k, 0], recv_sem=arecv.at[k, 0],
                device_id=(target, y), device_id_type=MESH,
            ).start()

    def rows_turn(k):
        seven = abuf.at[k, :, pl.ds(0, 56)]
        pltpu.make_async_copy(seven, seven, arecv.at[k, 0]).wait()
        for h in range(2):
            for i in range(NZ):
                bsrc[k, h, pl.ds(8 * i, 8)] = abuf[k, h, pl.ds(i, 8, stride=8)]
        bbuf[k, :, eight(z)] = bsrc[k, :, eight(z)]
        for i in range(1, NZ):
            other, target = mate_z(i)
            pltpu.make_async_remote_copy(
                src_ref=bsrc.at[k, :, eight(other)], dst_ref=bbuf.at[k, :, eight(z)],
                send_sem=asend.at[k, 1], recv_sem=arecv.at[k, 1],
                device_id=(target, y), device_id_type=MESH,
            ).start()

    def rows_in(k):
        seven = bbuf.at[k, :, pl.ds(0, 56)]
        pltpu.make_async_copy(seven, seven, arecv.at[k, 1]).wait()
        return jnp.concatenate([bbuf[k, 0], bbuf[k, 1]], axis=1)

    big_sub = lax.broadcasted_iota(jnp.int32, (128, 128), 0)
    big_lane = lax.broadcasted_iota(jnp.int32, (128, 128), 1)

    def split_m(p):
        def go():
            for n in (2 * p, 2 * p + 1):
                for g in range(GROUPS):
                    tile = mraw[g, :, pl.ds(128 * n, 128)]
                    mh[n, pl.ds(FACE * g, FACE)], ml[n, pl.ds(FACE * g, FACE)] = halves(tile)
        return go

    def turn_m(n):
        def go():
            same = (big_sub >> 6) == (big_lane >> 6)
            place = jnp.where(same & ((pairs[n : n + 1] >> 6) == (big_sub & 63)), 1.0, 0.0).astype(BF16)
            rows = dot_t(place, mh[n]) + dot_t(place, ml[n])
            for q in range(2):
                turned_m[q, pl.ds(128 * n, 128)] = rows[:, 128 * q : 128 * q + 128]
        return go

    equal = (
        lax.broadcasted_iota(jnp.int32, (256, 256), 0) == lax.broadcasted_iota(jnp.int32, (256, 256), 1)
    ).astype(F32).astype(BF16)

    def order_m(n):
        def go():
            slab = []
            for q in range(2):
                slab.append(jnp.concatenate([
                    turned_m[q, pl.ds(core * FACE + 2 * n + k, 32, stride=128)] for k in range(2) for core in range(2)
                ], axis=0))
            high, low = halves(jnp.concatenate(slab, axis=1))
            nh[n] = dot_t(equal, high).astype(BF16)
            nl[n] = dot_t(equal, low).astype(BF16)
        return go

    def split_k(d, r):
        def go():
            kh[d, pl.ds(128 * r, 128)], kl[d, pl.ds(128 * r, 128)] = halves(kraw[d, pl.ds(128 * r, 128)])
        return go

    def split_u(w2, d):
        def go():
            uh[d], ul[d] = halves(w2[d])
        return go

    def face_out(it, w):
        def go():
            for k, (src, target) in enumerate((
                (w.at[:, 7], (up, y)),
                (w.at[:, 0], (down, y)),
                (w.at[:, :, 7], (s, (y + 1) % GROUPS)),
                (w.at[:, :, 0], (s, (y + GROUPS - 1) % GROUPS)),
            )):
                pltpu.make_async_remote_copy(
                    src_ref=src, dst_ref=halo.at[it, k], send_sem=hsend.at[it], recv_sem=hrecv.at[it],
                    device_id=target, device_id_type=MESH,
                ).start()
        return go

    def face_in(it):
        def go():
            pltpu.make_async_copy(halo.at[it], halo.at[it], hrecv.at[it]).wait()
        return go

    low_i = jnp.where(s > 0, 1.0, 0.0).astype(F32)
    high_i = jnp.where(s < NX * NZ * NC - 1, 1.0, 0.0).astype(F32)
    low_j = jnp.where(y > 0, 1.0, 0.0).astype(F32)
    high_j = jnp.where(y < GROUPS - 1, 1.0, 0.0).astype(F32)
    weight = damping * coupling

    layer = lax.broadcasted_iota(jnp.int32, (32, EDGE, FIELDS), 1)

    def volume(w2, o2, d, r):
        def go():
            block = pl.ds(256 * r, 256)
            applied = dot3(kh[d, block], kl[d, block], uh[d], ul[d])
            here = w2[d, block].reshape(32, EDGE, FIELDS)
            term = here
            if d + 1 < DEPTH:
                term = here - pltpu.roll(w2[d + 1, block].reshape(32, EDGE, FIELDS), 7, 1)
            term = jnp.where(layer == EDGE - 1, term, 0.0)
            if d:
                above = here - pltpu.roll(w2[d - 1, block].reshape(32, EDGE, FIELDS), 1, 1)
                term = jnp.where(layer == 0, above, term)
            out = w2[d, block] + damping * (ld[d, block] - applied)
            o2[d, block] = out - weight * term.reshape(256, FIELDS)
        return go

    def faces(it, w, o, w2, o2, d):
        def go():
            o[d, 0] -= weight * (w[d, 0] - low_i * halo[it, 0, d])
            o[d, 7] -= weight * (w[d, 7] - high_i * halo[it, 1, d])
            o[d, :, 0] -= weight * (w[d, :, 0] - low_j * halo[it, 2, d])
            o[d, :, 7] -= weight * (w[d, :, 7] - high_j * halo[it, 3, d])
        return go

    x2 = xb.reshape(2, 2, 64 * FACE, 128)

    def boundary(it, spots):
        def go():
            left_h, left_l, right = [], [], []
            for dx, dz in spots:
                n = chip(-dx, -dz)
                left_h.append((mh if it else nh)[n])
                left_l.append((ml if it else nl)[n])
                rows = pl.ds(pl.multiple_of(128 * n, 128), 128)
                right.append(jnp.concatenate([x2[it, 0, rows], x2[it, 1, rows]], axis=1))
            xh, xl = halves(jnp.concatenate(right, axis=0))
            part[...] += dot3(jnp.concatenate(left_h, axis=1), jnp.concatenate(left_l, axis=1), xh, xl)
        return go

    def put_x(it, rows):
        for h in range(2):
            xb[it, h, s] = rows[:, 128 * h : 128 * h + 128]

    def gather(it, tasks, pops):
        tasks = list(tasks)
        xr = xb.at[it]

        def send(p, block, target):
            pltpu.make_async_remote_copy(
                src_ref=xr.at[:, block, PARTS[p]], dst_ref=xr.at[:, block, PARTS[p]],
                send_sem=gsend.at[it], recv_sem=grecv.at[it, p, block],
                device_id=(target, y), device_id_type=MESH,
            ).start()

        def wait(p, block):
            piece = xr.at[:, block, PARTS[p]]
            pltpu.make_async_copy(piece, piece, grecv.at[it, p, block]).wait()

        def share(block):
            pltpu.make_async_remote_copy(
                src_ref=xr.at[:, block], dst_ref=xr.at[:, block],
                send_sem=gsend.at[it], recv_sem=grecv.at[it, 0, block],
                device_id=(sibling, y), device_id_type=MESH,
            ).start()

        def shared(spots):
            def go():
                for dx, dz in spots:
                    block = at(-dx, -dz) + sgn
                    pltpu.make_async_copy(xr.at[:, block], xr.at[:, block], grecv.at[it, 0, block]).wait()
            return go

        def work(now, most):
            while tasks and tasks[0][0] <= now and most:
                tasks.pop(0)[1]()
                most -= 1

        for p, dx, dz in FIRST:
            send(p, s, at(dx, dz))
        share(s)
        part[...] = jnp.zeros_like(part)
        work(-1, pops)
        seen, fresh = {(0, 0): 2}, [(0, 0)]
        for now, (p, dx, dz, onward) in enumerate(ARRIVALS):
            block = at(-dx, -dz)
            wait(p, block)
            for tx, tz in onward:
                send(p, block, at(tx, tz))
            seen[dx, dz] = seen.get((dx, dz), 0) + 1
            if seen[dx, dz] == 2:
                share(block)
                fresh.append((dx, dz))
            if now >= START[it] and len(fresh) > LAG:
                early, fresh = fresh[:2], fresh[2:]
                tasks[:0] = [(0, shared(early)), (0, boundary(it, early))]
            work(now, pops)
        work(99, 99)
        shared(fresh)()
        for i in range(0, len(fresh), 4):
            boundary(it, fresh[i : i + 4])()

    def reduce(it, tasks):
        for i in (2, 1, 3):
            other = (y + i) % GROUPS
            pltpu.make_async_remote_copy(
                src_ref=part.at[pl.ds(pl.multiple_of(FACE * other, FACE), FACE)], dst_ref=rsbuf.at[it, i - 1],
                send_sem=rsend.at[it], recv_sem=rrecv.at[it],
                device_id=(s, other), device_id_type=MESH,
            ).start()
        for task in tasks:
            task()
        own = part[pl.ds(pl.multiple_of(FACE * y, FACE), FACE)]
        pltpu.make_async_copy(rsbuf.at[it], rsbuf.at[it], rrecv.at[it]).wait()
        total = own + rsbuf[it, 0] + rsbuf[it, 1] + rsbuf[it, 2]
        three = part.at[pl.ds(0, 3 * FACE)]
        pltpu.make_async_copy(three, three, rsend.at[it]).wait()
        return total

    lead.wait()
    put_x(0, exact(node_out, u2[0]))
    early = [rest.wait] + [copy.wait for copy in get_m] + [split_m(p) for p in range(16)] + [turn_m(n) for n in range(32)] + [order_m(n) for n in range(32)]
    later = [get_k.wait] + [split_u(u2, d) for d in range(3)]
    later += [split_k(0, r) for r in range(4)] + [get_l.wait] + [volume(u2, v2, 0, r) for r in range(2)]
    tasks = [(-1, task) for task in early[:13]] + [(0, task) for task in early[13:]]
    tasks[13:13] = [(3, face_out(0, u))]
    tasks += [(0, task) for task in later]
    tasks += [(36, face_in(0)), (36, faces(0, u, v, u2, v2, 0))]
    tasks += [(36, lambda: rows_out(1, exact(node_out, v2[0])))]
    for d in (1, 2):
        tasks += [(0, split_k(d, r)) for r in range(4)] + [(0, volume(u2, v2, d, r)) for r in range(2)]
        tasks += [(0, faces(0, u, v, u2, v2, d))]
    tasks += [(56, lambda: rows_turn(1))]
    gather(0, tasks, 4)
    traction = reduce(0, [])
    put_x(1, exact(slot_in, rows_in(1)) - damping * traction)
    tr[...] = traction

    def first_top():
        v2[0] -= damping * exact(node_in, rows_in(2))
        pltpu.make_async_copy(halo.at[0], halo.at[0], hsend.at[0]).wait()

    tasks = [(-1, lambda: rows_out(2, exact(slot_out, tr[...]))), (10, lambda: rows_turn(2))]
    tasks += [(22, first_top), (22, face_out(1, v))] + [(22, split_u(v2, d)) for d in range(3)]
    for d in (2, 1, 0):
        tasks += [(0, volume(v2, u2, d, r)) for r in range(2)]
    gather(1, tasks, 3)
    deep = pltpu.make_async_copy(u2.at[pl.ds(1, 2)], sol.at[pl.ds(1, 2)], osem.at[0])
    traction = reduce(1, [face_in(1)] + [faces(1, v, u, v2, u2, d) for d in (2, 1, 0)] + [deep.start])
    tr[...] = traction
    rows_out(3, exact(slot_out, traction))
    put_tr = pltpu.make_async_copy(tr, trac, osem.at[1])
    put_tr.start()
    rows_turn(3)
    u2[0] -= damping * exact(node_in, rows_in(3))
    last = pltpu.make_async_copy(u2.at[0], sol.at[0], osem.at[2])
    last.start()

    for it in range(2):
        most = xb.at[it, :, pl.ds(0, 63)]
        pltpu.make_async_copy(most, most, gsend.at[it]).wait()
    pltpu.make_async_copy(halo.at[1], halo.at[1], hsend.at[1]).wait()
    for k in (1, 2, 3):
        for phase in range(2):
            seven = abuf.at[k, :, pl.ds(0, 56)]
            pltpu.make_async_copy(seven, seven, asend.at[k, phase]).wait()
    deep.wait()
    put_tr.wait()
    last.wait()


def shards(stiffness, load, start, boundary_matrix, bem_node):
    anywhere = pl.BlockSpec(memory_space=pl.ANY)
    vmem = pl.BlockSpec(memory_space=pltpu.VMEM)
    dma = pltpu.SemaphoreType.DMA
    field = (DEPTH, EDGE, EDGE, EDGE, FIELDS)
    flat = (DEPTH, NODES, FIELDS)
    sol, trac = pl.pallas_call(
        kernel,
        out_shape=(
            jax.ShapeDtypeStruct(flat, F32),
            jax.ShapeDtypeStruct((FACE, FIELDS), F32),
        ),
        in_specs=[anywhere] * 4 + [vmem],
        out_specs=(anywhere, anywhere),
        scratch_shapes=[
            pltpu.VMEM(field, F32), pltpu.VMEM(field, F32), pltpu.VMEM(flat, F32),
            pltpu.VMEM(flat, BF16), pltpu.VMEM(flat, BF16),
            pltpu.VMEM((DEPTH, NODES, NODES), F32),
            pltpu.VMEM((DEPTH, NODES, NODES), BF16), pltpu.VMEM((DEPTH, NODES, NODES), BF16),
            pltpu.VMEM((GROUPS, FACE, COLS), F32),
            *[pltpu.VMEM((32, 256, 128), BF16)] * 4,
            pltpu.VMEM((2, COLS, 128), F32),
            pltpu.VMEM((2, 2, 64, FACE, 128), F32),
            pltpu.VMEM((256, FIELDS), F32),
            pltpu.VMEM((2, 3, FACE, FIELDS), F32),
            pltpu.VMEM((2, 4, DEPTH, EDGE, EDGE, FIELDS), F32),
            pltpu.VMEM((FACE, FIELDS), F32),
            *[pltpu.VMEM((4, 2, FACE, 128), F32)] * 4,
            dma((9,)), dma((2,)), dma((2, 2, 64)), dma((4, 2)), dma((4, 2)),
            dma((2,)), dma((2,)), dma((2,)), dma((2,)), dma((3,)),
        ],
        compiler_params=pltpu.CompilerParams(
            collective_id=0, has_side_effects=True, vmem_limit_bytes=58 * 2**20
        ),
        name="interface_iterations",
    )(stiffness[0], load[0], start[0], boundary_matrix, bem_node.reshape(32, 128))
    return sol[None], trac[None]


def solution(mesh):
    in_specs = (
        P(("surf", "col"), None, None, None),
        P(("surf", "col"), None, None, None),
        P(("surf", "col"), None, None, None),
        P("surf", None, "col"),
        P("col", None),
    )
    out_specs = (P(("surf", "col"), None, None, None), P("col", "surf", None))
    return jax.shard_map(shards, mesh=mesh, in_specs=in_specs, out_specs=out_specs, check_vma=False)
```

```python
import functools

import jax
import jax.numpy as jnp
from jax import lax
from jax.experimental import pallas as pl
from jax.experimental.pallas import tpu as pltpu
from jax.sharding import PartitionSpec as P

MESH = pl.DeviceIdType.MESH
F32, BF16 = jnp.float32, jnp.bfloat16
START = (30, 12)
LAG = 8
NX, NZ, NC = 4, 8, 2
EDGE, DEPTH, NODES, FACE, FIELDS = 8, 3, 512, 64, 256
GROUPS, COLS = 4, 4096
SPLIT = 24
PARTS = (pl.ds(0, SPLIT), pl.ds(SPLIT, FACE - SPLIT))
damping = 0.25
coupling = 0.5


FIRST = (
    (0, 0, 1), (1, 0, -2), (1, 0, -1), (1, 0, 2), (0, 1, 0), (1, 0, 1), (0, 0, -2), (1, -1, 0), (0, -1, 0), (1, 1, 0),
)
ARRIVALS = (
    (0, 1, 0, ((0, -1), (1, 0))), (0, 0, 1, ((0, 2), (1, 0), (-1, 0))),
    (1, -1, 0, ((0, 1), (-1, 0))), (1, 1, 0, ()),
    (0, -1, 0, ()), (1, 0, -2, ((0, -1), (0, -2), (1, 0))),
    (1, 0, 2, ((-1, 0), (1, 0))), (1, 0, -1, ((-1, 0), (1, 0))),
    (1, 0, 1, ((1, 0),)), (0, 2, 0, ((0, 1),)),
    (0, -1, 1, ((0, 1),)), (0, 0, -2, ((0, -1), (1, 0), (0, 1), (-1, 0))),
    (0, 1, 1, ((0, 1),)), (0, 1, -1, ((1, 0),)),
    (0, 0, 3, ((-1, 0), (0, 1))), (1, 2, 0, ()),
    (1, 1, -2, ()), (1, 0, -3, ((-1, 0), (1, 0))),
    (1, -1, 1, ()), (1, -1, 2, ((-1, 0),)),
    (1, 1, 2, ((0, 1),)), (1, -1, -1, ((-1, 0),)),
    (1, 0, 4, ((0, -1), (1, 0))), (1, 1, -1, ()),
    (0, -1, -2, ()), (0, -1, 3, ((-1, 0), (0, 1))),
    (1, 1, 1, ((1, 0),)), (0, 2, 1, ()),
    (0, 1, -2, ((0, -1), (1, 0))), (0, -1, 2, ()),
    (1, -1, -3, ((0, 1), (0, -1), (-1, 0))), (0, 2, -1, ((1, 0), (0, -2))),
    (0, 0, -1, ()), (1, 2, 2, ((0, 1),)),
    (1, 1, -3, ()), (0, 1, 2, ((-1, 0), (0, 1), (1, 0))),
    (0, 0, -3, ((-1, 0),)), (0, 0, 4, ((1, 0),)),
    (1, 2, -1, ((0, -1),)), (1, 1, 4, ((1, 0),)),
    (1, 0, 3, ((-1, 0),)), (0, 2, 3, ((0, 1),)),
    (1, 1, 3, ()), (1, 2, 1, ()),
    (0, 1, -3, ()), (0, -1, 4, ()),
    (0, 2, -2, ()), (1, 2, -3, ()),
    (1, -1, 4, ()), (0, -1, -1, ()),
    (1, -1, -2, ()), (0, 0, 2, ()),
    (0, 2, 2, ()), (0, -1, -3, ()),
    (1, 2, 3, ()), (0, 2, -3, ()),
    (0, 1, 4, ()), (0, 1, 3, ()),
    (1, -1, 3, ()), (1, 2, -2, ()),
    (1, 2, 4, ()), (0, 2, 4, ()),
)


def halves(a):
    high = a.astype(BF16)
    return high, (a - high.astype(F32)).astype(BF16)


def dot(a, b):
    return jnp.dot(a, b, preferred_element_type=F32)


def dot_t(a, b):
    return lax.dot_general(a, b, (((1,), (1,)), ((), ())), preferred_element_type=F32)


def dot3(ah, al, bh, bl):
    return dot(ah, bh) + dot(al, bh) + dot(ah, bl)


def exact(onehot, rows):
    high, low = halves(rows)
    least = (rows - high.astype(F32) - low.astype(F32)).astype(BF16)
    return dot(onehot, high) + dot(onehot, low) + dot(onehot, least)


def kernel(
    stiff, load, start, bm, nodes, sol, trac,
    u, v, ld, uh, ul, kraw, kh, kl, mraw, mh, ml, nh, nl, turned_m, xb, part, rsbuf, halo, tr,
    asrc, abuf, bsrc, bbuf,
    lsem, gsend, grecv, asend, arecv, rsend, rrecv, hsend, hrecv, osem,
):
    s, y = lax.axis_index("surf"), lax.axis_index("col")
    c, z, x = s % NC, (s // NC) % NZ, s // (NC * NZ)
    sgn = 1 - 2 * c
    xc = c * NX + x
    u2, v2 = u.reshape(DEPTH, NODES, FIELDS), v.reshape(DEPTH, NODES, FIELDS)

    def at(dx, dz):
        return ((x + NX + dx) % NX * NZ + (z + NZ + dz) % NZ) * NC + c

    def chip(dx, dz):
        return (x + NX + dx) % NX * NZ + (z + NZ + dz) % NZ

    sibling = s + sgn
    up, down = (s + 1) % (NX * NZ * NC), (s + NX * NZ * NC - 1) % (NX * NZ * NC)

    def mate_xc(i):
        other = (xc + i) % (NX * NC)
        return other, (other % NX * NZ + z) * NC + other // NX

    def mate_z(i):
        other = (z + i) % NZ
        return other, (x * NZ + other) * NC + c

    lead = pltpu.make_async_copy(start.at[0], u2.at[0], lsem.at[0])
    rest = pltpu.make_async_copy(start.at[pl.ds(1, 2)], u2.at[pl.ds(1, 2)], lsem.at[1])
    get_m = [pltpu.make_async_copy(bm.at[:, g], mraw.at[g], lsem.at[5 + g]) for g in range(GROUPS)]
    get_k = pltpu.make_async_copy(stiff, kraw, lsem.at[3])
    get_l = pltpu.make_async_copy(load, ld, lsem.at[4])
    for copy in (lead, *get_m, rest, get_k, get_l):
        copy.start()

    barrier = pltpu.get_barrier_semaphore()

    def greet(surf, col):
        pl.semaphore_signal(barrier, inc=1, device_id=(surf, col), device_id_type=MESH)

    for i in range(1, NX * NC):
        greet(mate_xc(i)[1], y)
    for i in range(1, NZ):
        greet(mate_z(i)[1], y)
    for i in range(1, GROUPS):
        greet(s, (y + i) % GROUPS)
    greet((s + NX * NZ * NC - sgn) % (NX * NZ * NC), y)

    sub = lax.broadcasted_iota(jnp.int32, (FACE, FACE), 0)
    lane = lax.broadcasted_iota(jnp.int32, (FACE, FACE), 1)
    pairs = nodes[...]
    held = jnp.concatenate([pairs[:, :FACE], pairs[:, FACE:]], axis=0)
    mine = jnp.sum(jnp.where((held >> 6) == s, held & 63, 0), axis=1, keepdims=True)
    lane_8 = lax.broadcasted_iota(jnp.int32, (FACE, NODES), 1)
    node_out = (mine * EDGE == lane_8).astype(F32).astype(BF16)
    turned = jnp.sum(jnp.where(sub == (lane & 7) * 8 + (lane >> 3), mine, 0), axis=0, keepdims=True)
    sub_8 = lax.broadcasted_iota(jnp.int32, (NODES, FACE), 0)
    node_in = (turned * EDGE == sub_8).astype(F32).astype(BF16)
    patch = jnp.sum(jnp.where(sub == xc * NZ + z, held, 0), axis=0, keepdims=True) >> 6
    slot_out = ((patch & 1) * 32 + (patch >> 1) == sub).astype(F32).astype(BF16)
    column = jnp.sum(jnp.where(sub == lane, patch, 0), axis=1, keepdims=True)
    slot_in = (((column >> 1) & 7) * 8 + (column & 1) * NX + (column >> 4) == lane).astype(F32).astype(BF16)

    def eight(i):
        return pl.ds(pl.multiple_of(i * 8, 8), 8)

    def rows_out(k, rows):
        for h in range(2):
            asrc[k, h] = rows[:, 128 * h : 128 * h + 128]
        abuf[k, :, eight(xc)] = asrc[k, :, eight(xc)]
        for i in range(1, NX * NC):
            other, target = mate_xc(i)
            pltpu.make_async_remote_copy(
                src_ref=asrc.at[k, :, eight(other)], dst_ref=abuf.at[k, :, eight(xc)],
                send_sem=asend.at[k, 0], recv_sem=arecv.at[k, 0],
                device_id=(target, y), device_id_type=MESH,
            ).start()

    def rows_turn(k):
        seven = abuf.at[k, :, pl.ds(0, 56)]
        pltpu.make_async_copy(seven, seven, arecv.at[k, 0]).wait()
        for h in range(2):
            for i in range(NZ):
                bsrc[k, h, pl.ds(8 * i, 8)] = abuf[k, h, pl.ds(i, 8, stride=8)]
        bbuf[k, :, eight(z)] = bsrc[k, :, eight(z)]
        for i in range(1, NZ):
            other, target = mate_z(i)
            pltpu.make_async_remote_copy(
                src_ref=bsrc.at[k, :, eight(other)], dst_ref=bbuf.at[k, :, eight(z)],
                send_sem=asend.at[k, 1], recv_sem=arecv.at[k, 1],
                device_id=(target, y), device_id_type=MESH,
            ).start()

    def rows_in(k):
        seven = bbuf.at[k, :, pl.ds(0, 56)]
        pltpu.make_async_copy(seven, seven, arecv.at[k, 1]).wait()
        return jnp.concatenate([bbuf[k, 0], bbuf[k, 1]], axis=1)

    big_sub = lax.broadcasted_iota(jnp.int32, (128, 128), 0)
    big_lane = lax.broadcasted_iota(jnp.int32, (128, 128), 1)

    def split_m(p):
        def go():
            for n in (2 * p, 2 * p + 1):
                for g in range(GROUPS):
                    tile = mraw[g, :, pl.ds(128 * n, 128)]
                    mh[n, pl.ds(FACE * g, FACE)], ml[n, pl.ds(FACE * g, FACE)] = halves(tile)
        return go

    def turn_m(n):
        def go():
            same = (big_sub >> 6) == (big_lane >> 6)
            place = jnp.where(same & ((pairs[n : n + 1] >> 6) == (big_sub & 63)), 1.0, 0.0).astype(BF16)
            rows = dot_t(place, mh[n]) + dot_t(place, ml[n])
            for q in range(2):
                turned_m[q, pl.ds(128 * n, 128)] = rows[:, 128 * q : 128 * q + 128]
        return go

    equal = (
        lax.broadcasted_iota(jnp.int32, (256, 256), 0) == lax.broadcasted_iota(jnp.int32, (256, 256), 1)
    ).astype(F32).astype(BF16)

    def order_m(n):
        def go():
            slab = []
            for q in range(2):
                slab.append(jnp.concatenate([
                    turned_m[q, pl.ds(core * FACE + 2 * n + k, 32, stride=128)] for k in range(2) for core in range(2)
                ], axis=0))
            high, low = halves(jnp.concatenate(slab, axis=1))
            nh[n] = dot_t(equal, high).astype(BF16)
            nl[n] = dot_t(equal, low).astype(BF16)
        return go

    def split_k(d, r):
        def go():
            kh[d, pl.ds(128 * r, 128)], kl[d, pl.ds(128 * r, 128)] = halves(kraw[d, pl.ds(128 * r, 128)])
        return go

    def split_u(w2, d):
        def go():
            uh[d], ul[d] = halves(w2[d])
        return go

    def face_out(it, w):
        def go():
            for k, (src, target) in enumerate((
                (w.at[:, 7], (up, y)),
                (w.at[:, 0], (down, y)),
                (w.at[:, :, 7], (s, (y + 1) % GROUPS)),
                (w.at[:, :, 0], (s, (y + GROUPS - 1) % GROUPS)),
            )):
                pltpu.make_async_remote_copy(
                    src_ref=src, dst_ref=halo.at[it, k], send_sem=hsend.at[it], recv_sem=hrecv.at[it],
                    device_id=target, device_id_type=MESH,
                ).start()
        return go

    def face_in(it):
        def go():
            pltpu.make_async_copy(halo.at[it], halo.at[it], hrecv.at[it]).wait()
        return go

    low_i = jnp.where(s > 0, 1.0, 0.0).astype(F32)
    high_i = jnp.where(s < NX * NZ * NC - 1, 1.0, 0.0).astype(F32)
    low_j = jnp.where(y > 0, 1.0, 0.0).astype(F32)
    high_j = jnp.where(y < GROUPS - 1, 1.0, 0.0).astype(F32)
    weight = damping * coupling

    layer = lax.broadcasted_iota(jnp.int32, (32, EDGE, FIELDS), 1)

    def volume(w2, o2, d, r):
        def go():
            block = pl.ds(256 * r, 256)
            applied = dot3(kh[d, block], kl[d, block], uh[d], ul[d])
            here = w2[d, block].reshape(32, EDGE, FIELDS)
            term = here
            if d + 1 < DEPTH:
                term = here - pltpu.roll(w2[d + 1, block].reshape(32, EDGE, FIELDS), 7, 1)
            term = jnp.where(layer == EDGE - 1, term, 0.0)
            if d:
                above = here - pltpu.roll(w2[d - 1, block].reshape(32, EDGE, FIELDS), 1, 1)
                term = jnp.where(layer == 0, above, term)
            out = w2[d, block] + damping * (ld[d, block] - applied)
            o2[d, block] = out - weight * term.reshape(256, FIELDS)
        return go

    def faces(it, w, o, w2, o2, d):
        def go():
            o[d, 0] -= weight * (w[d, 0] - low_i * halo[it, 0, d])
            o[d, 7] -= weight * (w[d, 7] - high_i * halo[it, 1, d])
            o[d, :, 0] -= weight * (w[d, :, 0] - low_j * halo[it, 2, d])
            o[d, :, 7] -= weight * (w[d, :, 7] - high_j * halo[it, 3, d])
        return go

    x2 = xb.reshape(2, 2, 64 * FACE, 128)

    def boundary(it, spots):
        def go():
            left_h, left_l, right = [], [], []
            for dx, dz in spots:
                n = chip(-dx, -dz)
                left_h.append((mh if it else nh)[n])
                left_l.append((ml if it else nl)[n])
                rows = pl.ds(pl.multiple_of(128 * n, 128), 128)
                right.append(jnp.concatenate([x2[it, 0, rows], x2[it, 1, rows]], axis=1))
            xh, xl = halves(jnp.concatenate(right, axis=0))
            part[...] += dot3(jnp.concatenate(left_h, axis=1), jnp.concatenate(left_l, axis=1), xh, xl)
        return go

    def put_x(it, rows):
        for h in range(2):
            xb[it, h, s] = rows[:, 128 * h : 128 * h + 128]

    def gather(it, tasks, pops):
        tasks = list(tasks)
        xr = xb.at[it]

        def send(p, block, target):
            pltpu.make_async_remote_copy(
                src_ref=xr.at[:, block, PARTS[p]], dst_ref=xr.at[:, block, PARTS[p]],
                send_sem=gsend.at[it], recv_sem=grecv.at[it, p, block],
                device_id=(target, y), device_id_type=MESH,
            ).start()

        def wait(p, block):
            piece = xr.at[:, block, PARTS[p]]
            pltpu.make_async_copy(piece, piece, grecv.at[it, p, block]).wait()

        def share(block):
            pltpu.make_async_remote_copy(
                src_ref=xr.at[:, block], dst_ref=xr.at[:, block],
                send_sem=gsend.at[it], recv_sem=grecv.at[it, 0, block],
                device_id=(sibling, y), device_id_type=MESH,
            ).start()

        def shared(spots):
            def go():
                for dx, dz in spots:
                    block = at(-dx, -dz) + sgn
                    pltpu.make_async_copy(xr.at[:, block], xr.at[:, block], grecv.at[it, 0, block]).wait()
            return go

        def work(now, most):
            while tasks and tasks[0][0] <= now and most:
                tasks.pop(0)[1]()
                most -= 1

        for p, dx, dz in FIRST:
            send(p, s, at(dx, dz))
        share(s)
        part[...] = jnp.zeros_like(part)
        work(-1, pops)
        seen, fresh = {(0, 0): 2}, [(0, 0)]
        for now, (p, dx, dz, onward) in enumerate(ARRIVALS):
            block = at(-dx, -dz)
            wait(p, block)
            for tx, tz in onward:
                send(p, block, at(tx, tz))
            seen[dx, dz] = seen.get((dx, dz), 0) + 1
            if seen[dx, dz] == 2:
                share(block)
                fresh.append((dx, dz))
            if now >= START[it] and len(fresh) > LAG:
                early, fresh = fresh[:2], fresh[2:]
                tasks[:0] = [(0, shared(early)), (0, boundary(it, early))]
            work(now, pops)
        work(99, 99)
        shared(fresh)()
        for i in range(0, len(fresh), 4):
            boundary(it, fresh[i : i + 4])()

    def reduce(it, tasks):
        for i in (2, 1, 3):
            other = (y + i) % GROUPS
            pltpu.make_async_remote_copy(
                src_ref=part.at[pl.ds(pl.multiple_of(FACE * other, FACE), FACE)], dst_ref=rsbuf.at[it, i - 1],
                send_sem=rsend.at[it], recv_sem=rrecv.at[it],
                device_id=(s, other), device_id_type=MESH,
            ).start()
        for task in tasks:
            task()
        own = part[pl.ds(pl.multiple_of(FACE * y, FACE), FACE)]
        pltpu.make_async_copy(rsbuf.at[it], rsbuf.at[it], rrecv.at[it]).wait()
        total = own + rsbuf[it, 0] + rsbuf[it, 1] + rsbuf[it, 2]
        three = part.at[pl.ds(0, 3 * FACE)]
        pltpu.make_async_copy(three, three, rsend.at[it]).wait()
        return total

    lead.wait()
    put_x(0, exact(node_out, u2[0]))
    pl.semaphore_wait(barrier, NX * NC - 1 + NZ - 1 + GROUPS - 1 + 1)
    early = [rest.wait] + [copy.wait for copy in get_m] + [split_m(p) for p in range(16)] + [turn_m(n) for n in range(32)] + [order_m(n) for n in range(32)]
    later = [get_k.wait] + [split_u(u2, d) for d in range(3)]
    later += [split_k(0, r) for r in range(4)] + [get_l.wait] + [volume(u2, v2, 0, r) for r in range(2)]
    tasks = [(-1, task) for task in early[:13]] + [(0, task) for task in early[13:]]
    tasks[13:13] = [(3, face_out(0, u))]
    tasks += [(0, task) for task in later]
    tasks += [(36, face_in(0)), (36, faces(0, u, v, u2, v2, 0))]
    tasks += [(36, lambda: rows_out(1, exact(node_out, v2[0])))]
    for d in (1, 2):
        tasks += [(0, split_k(d, r)) for r in range(4)] + [(0, volume(u2, v2, d, r)) for r in range(2)]
        tasks += [(0, faces(0, u, v, u2, v2, d))]
    tasks += [(56, lambda: rows_turn(1))]
    gather(0, tasks, 4)
    traction = reduce(0, [])
    put_x(1, exact(slot_in, rows_in(1)) - damping * traction)
    tr[...] = traction

    def first_top():
        v2[0] -= damping * exact(node_in, rows_in(2))
        pltpu.make_async_copy(halo.at[0], halo.at[0], hsend.at[0]).wait()

    tasks = [(-1, lambda: rows_out(2, exact(slot_out, tr[...]))), (10, lambda: rows_turn(2))]
    tasks += [(22, first_top), (22, face_out(1, v))] + [(22, split_u(v2, d)) for d in range(3)]
    for d in (2, 1, 0):
        tasks += [(0, volume(v2, u2, d, r)) for r in range(2)]
    gather(1, tasks, 3)
    deep = pltpu.make_async_copy(u2.at[pl.ds(1, 2)], sol.at[pl.ds(1, 2)], osem.at[0])
    traction = reduce(1, [])
    tr[...] = traction
    rows_out(3, exact(slot_out, traction))
    put_tr = pltpu.make_async_copy(tr, trac, osem.at[1])
    put_tr.start()
    rows_turn(3)
    for task in [face_in(1)] + [faces(1, v, u, v2, u2, d) for d in (2, 1, 0)] + [deep.start]:
        task()
    u2[0] -= damping * exact(node_in, rows_in(3))
    last = pltpu.make_async_copy(u2.at[0], sol.at[0], osem.at[2])
    last.start()

    for it in range(2):
        most = xb.at[it, :, pl.ds(0, 63)]
        pltpu.make_async_copy(most, most, gsend.at[it]).wait()
    pltpu.make_async_copy(halo.at[1], halo.at[1], hsend.at[1]).wait()
    for k in (1, 2, 3):
        for phase in range(2):
            seven = abuf.at[k, :, pl.ds(0, 56)]
            pltpu.make_async_copy(seven, seven, asend.at[k, phase]).wait()
    deep.wait()
    put_tr.wait()
    last.wait()


def shards(stiffness, load, start, boundary_matrix, bem_node):
    anywhere = pl.BlockSpec(memory_space=pl.ANY)
    vmem = pl.BlockSpec(memory_space=pltpu.VMEM)
    dma = pltpu.SemaphoreType.DMA
    field = (DEPTH, EDGE, EDGE, EDGE, FIELDS)
    flat = (DEPTH, NODES, FIELDS)
    sol, trac = pl.pallas_call(
        kernel,
        out_shape=(
            jax.ShapeDtypeStruct(flat, F32),
            jax.ShapeDtypeStruct((FACE, FIELDS), F32),
        ),
        in_specs=[anywhere] * 4 + [vmem],
        out_specs=(anywhere, anywhere),
        scratch_shapes=[
            pltpu.VMEM(field, F32), pltpu.VMEM(field, F32), pltpu.VMEM(flat, F32),
            pltpu.VMEM(flat, BF16), pltpu.VMEM(flat, BF16),
            pltpu.VMEM((DEPTH, NODES, NODES), F32),
            pltpu.VMEM((DEPTH, NODES, NODES), BF16), pltpu.VMEM((DEPTH, NODES, NODES), BF16),
            pltpu.VMEM((GROUPS, FACE, COLS), F32),
            *[pltpu.VMEM((32, 256, 128), BF16)] * 4,
            pltpu.VMEM((2, COLS, 128), F32),
            pltpu.VMEM((2, 2, 64, FACE, 128), F32),
            pltpu.VMEM((256, FIELDS), F32),
            pltpu.VMEM((2, 3, FACE, FIELDS), F32),
            pltpu.VMEM((2, 4, DEPTH, EDGE, EDGE, FIELDS), F32),
            pltpu.VMEM((FACE, FIELDS), F32),
            *[pltpu.VMEM((4, 2, FACE, 128), F32)] * 4,
            dma((9,)), dma((2,)), dma((2, 2, 64)), dma((4, 2)), dma((4, 2)),
            dma((2,)), dma((2,)), dma((2,)), dma((2,)), dma((3,)),
        ],
        compiler_params=pltpu.CompilerParams(
            collective_id=0, has_side_effects=True, vmem_limit_bytes=58 * 2**20
        ),
        name="interface_iterations",
    )(stiffness[0], load[0], start[0], boundary_matrix, bem_node.reshape(32, 128))
    return sol[None], trac[None]


def solution(mesh):
    in_specs = (
        P(("surf", "col"), None, None, None),
        P(("surf", "col"), None, None, None),
        P(("surf", "col"), None, None, None),
        P("surf", None, "col"),
        P("col", None),
    )
    out_specs = (P(("surf", "col"), None, None, None), P("col", "surf", None))
    return jax.shard_map(shards, mesh=mesh, in_specs=in_specs, out_specs=out_specs, check_vma=False)
```

```python
import functools

import jax
import jax.numpy as jnp
from jax import lax
from jax.experimental import pallas as pl
from jax.experimental.pallas import tpu as pltpu
from jax.sharding import PartitionSpec as P

MESH = pl.DeviceIdType.MESH
F32, BF16 = jnp.float32, jnp.bfloat16
START = (30, 12)
LAG = 5
NX, NZ, NC = 4, 8, 2
EDGE, DEPTH, NODES, FACE, FIELDS = 8, 3, 512, 64, 256
GROUPS, COLS = 4, 4096
SPLIT = 24
PARTS = (pl.ds(0, SPLIT), pl.ds(SPLIT, FACE - SPLIT))
damping = 0.25
coupling = 0.5


FIRST = (
    (0, 0, 1), (1, 0, -2), (1, 0, -1), (1, 0, 2), (0, 1, 0), (1, 0, 1), (0, 0, -2), (1, -1, 0), (0, -1, 0), (1, 1, 0),
)
ARRIVALS = (
    (0, 1, 0, ((0, -1), (1, 0))), (0, 0, 1, ((0, 2), (1, 0), (-1, 0))),
    (1, -1, 0, ((0, 1), (-1, 0))), (1, 1, 0, ()),
    (0, -1, 0, ()), (1, 0, -2, ((0, -1), (0, -2), (1, 0))),
    (1, 0, 2, ((-1, 0), (1, 0))), (1, 0, -1, ((-1, 0), (1, 0))),
    (1, 0, 1, ((1, 0),)), (0, 2, 0, ((0, 1),)),
    (0, -1, 1, ((0, 1),)), (0, 0, -2, ((0, -1), (1, 0), (0, 1), (-1, 0))),
    (0, 1, 1, ((0, 1),)), (0, 1, -1, ((1, 0),)),
    (0, 0, 3, ((-1, 0), (0, 1))), (1, 2, 0, ()),
    (1, 1, -2, ()), (1, 0, -3, ((-1, 0), (1, 0))),
    (1, -1, 1, ()), (1, -1, 2, ((-1, 0),)),
    (1, 1, 2, ((0, 1),)), (1, -1, -1, ((-1, 0),)),
    (1, 0, 4, ((0, -1), (1, 0))), (1, 1, -1, ()),
    (0, -1, -2, ()), (0, -1, 3, ((-1, 0), (0, 1))),
    (1, 1, 1, ((1, 0),)), (0, 2, 1, ()),
    (0, 1, -2, ((0, -1), (1, 0))), (0, -1, 2, ()),
    (1, -1, -3, ((0, 1), (0, -1), (-1, 0))), (0, 2, -1, ((1, 0), (0, -2))),
    (0, 0, -1, ()), (1, 2, 2, ((0, 1),)),
    (1, 1, -3, ()), (0, 1, 2, ((-1, 0), (0, 1), (1, 0))),
    (0, 0, -3, ((-1, 0),)), (0, 0, 4, ((1, 0),)),
    (1, 2, -1, ((0, -1),)), (1, 1, 4, ((1, 0),)),
    (1, 0, 3, ((-1, 0),)), (0, 2, 3, ((0, 1),)),
    (1, 1, 3, ()), (1, 2, 1, ()),
    (0, 1, -3, ()), (0, -1, 4, ()),
    (0, 2, -2, ()), (1, 2, -3, ()),
    (1, -1, 4, ()), (0, -1, -1, ()),
    (1, -1, -2, ()), (0, 0, 2, ()),
    (0, 2, 2, ()), (0, -1, -3, ()),
    (1, 2, 3, ()), (0, 2, -3, ()),
    (0, 1, 4, ()), (0, 1, 3, ()),
    (1, -1, 3, ()), (1, 2, -2, ()),
    (1, 2, 4, ()), (0, 2, 4, ()),
)


def halves(a):
    high = a.astype(BF16)
    return high, (a - high.astype(F32)).astype(BF16)


def dot(a, b):
    return jnp.dot(a, b, preferred_element_type=F32)


def dot_t(a, b):
    return lax.dot_general(a, b, (((1,), (1,)), ((), ())), preferred_element_type=F32)


def dot3(ah, al, bh, bl):
    return dot(ah, bh) + dot(al, bh) + dot(ah, bl)


def exact(onehot, rows):
    high, low = halves(rows)
    least = (rows - high.astype(F32) - low.astype(F32)).astype(BF16)
    return dot(onehot, high) + dot(onehot, low) + dot(onehot, least)


def kernel(
    stiff, load, start, bm, nodes, sol, trac,
    u, v, ld, uh, ul, kraw, kh, kl, mraw, mh, ml, nh, nl, turned_m, xb, part, rsbuf, halo, tr,
    asrc, abuf, bsrc, bbuf,
    lsem, gsend, grecv, asend, arecv, rsend, rrecv, hsend, hrecv, osem,
):
    s, y = lax.axis_index("surf"), lax.axis_index("col")
    c, z, x = s % NC, (s // NC) % NZ, s // (NC * NZ)
    sgn = 1 - 2 * c
    xc = c * NX + x
    u2, v2 = u.reshape(DEPTH, NODES, FIELDS), v.reshape(DEPTH, NODES, FIELDS)

    def at(dx, dz):
        return ((x + NX + dx) % NX * NZ + (z + NZ + dz) % NZ) * NC + c

    def chip(dx, dz):
        return (x + NX + dx) % NX * NZ + (z + NZ + dz) % NZ

    sibling = s + sgn
    up, down = (s + 1) % (NX * NZ * NC), (s + NX * NZ * NC - 1) % (NX * NZ * NC)

    def mate_xc(i):
        other = (xc + i) % (NX * NC)
        return other, (other % NX * NZ + z) * NC + other // NX

    def mate_z(i):
        other = (z + i) % NZ
        return other, (x * NZ + other) * NC + c

    lead = pltpu.make_async_copy(start.at[0], u2.at[0], lsem.at[0])
    rest = pltpu.make_async_copy(start.at[pl.ds(1, 2)], u2.at[pl.ds(1, 2)], lsem.at[1])
    get_m = [pltpu.make_async_copy(bm.at[:, g], mraw.at[g], lsem.at[5 + g]) for g in range(GROUPS)]
    get_k = pltpu.make_async_copy(stiff, kraw, lsem.at[3])
    get_l = pltpu.make_async_copy(load, ld, lsem.at[4])
    for copy in (lead, *get_m, rest, get_k, get_l):
        copy.start()

    barrier = pltpu.get_barrier_semaphore()

    def greet(surf, col):
        pl.semaphore_signal(barrier, inc=1, device_id=(surf, col), device_id_type=MESH)

    for i in range(1, NX * NC):
        greet(mate_xc(i)[1], y)
    for i in range(1, NZ):
        greet(mate_z(i)[1], y)
    for i in range(1, GROUPS):
        greet(s, (y + i) % GROUPS)
    greet((s + NX * NZ * NC - sgn) % (NX * NZ * NC), y)

    sub = lax.broadcasted_iota(jnp.int32, (FACE, FACE), 0)
    lane = lax.broadcasted_iota(jnp.int32, (FACE, FACE), 1)
    pairs = nodes[...]
    held = jnp.concatenate([pairs[:, :FACE], pairs[:, FACE:]], axis=0)
    mine = jnp.sum(jnp.where((held >> 6) == s, held & 63, 0), axis=1, keepdims=True)
    lane_8 = lax.broadcasted_iota(jnp.int32, (FACE, NODES), 1)
    node_out = (mine * EDGE == lane_8).astype(F32).astype(BF16)
    turned = jnp.sum(jnp.where(sub == (lane & 7) * 8 + (lane >> 3), mine, 0), axis=0, keepdims=True)
    sub_8 = lax.broadcasted_iota(jnp.int32, (NODES, FACE), 0)
    node_in = (turned * EDGE == sub_8).astype(F32).astype(BF16)
    patch = jnp.sum(jnp.where(sub == xc * NZ + z, held, 0), axis=0, keepdims=True) >> 6
    slot_out = ((patch & 1) * 32 + (patch >> 1) == sub).astype(F32).astype(BF16)
    column = jnp.sum(jnp.where(sub == lane, patch, 0), axis=1, keepdims=True)
    slot_in = (((column >> 1) & 7) * 8 + (column & 1) * NX + (column >> 4) == lane).astype(F32).astype(BF16)

    def eight(i):
        return pl.ds(pl.multiple_of(i * 8, 8), 8)

    def rows_out(k, rows):
        for h in range(2):
            asrc[k, h] = rows[:, 128 * h : 128 * h + 128]
        abuf[k, :, eight(xc)] = asrc[k, :, eight(xc)]
        for i in range(1, NX * NC):
            other, target = mate_xc(i)
            pltpu.make_async_remote_copy(
                src_ref=asrc.at[k, :, eight(other)], dst_ref=abuf.at[k, :, eight(xc)],
                send_sem=asend.at[k, 0], recv_sem=arecv.at[k, 0],
                device_id=(target, y), device_id_type=MESH,
            ).start()

    def rows_turn(k):
        seven = abuf.at[k, :, pl.ds(0, 56)]
        pltpu.make_async_copy(seven, seven, arecv.at[k, 0]).wait()
        for h in range(2):
            for i in range(NZ):
                bsrc[k, h, pl.ds(8 * i, 8)] = abuf[k, h, pl.ds(i, 8, stride=8)]
        bbuf[k, :, eight(z)] = bsrc[k, :, eight(z)]
        for i in range(1, NZ):
            other, target = mate_z(i)
            pltpu.make_async_remote_copy(
                src_ref=bsrc.at[k, :, eight(other)], dst_ref=bbuf.at[k, :, eight(z)],
                send_sem=asend.at[k, 1], recv_sem=arecv.at[k, 1],
                device_id=(target, y), device_id_type=MESH,
            ).start()

    def rows_in(k):
        seven = bbuf.at[k, :, pl.ds(0, 56)]
        pltpu.make_async_copy(seven, seven, arecv.at[k, 1]).wait()
        return jnp.concatenate([bbuf[k, 0], bbuf[k, 1]], axis=1)

    big_sub = lax.broadcasted_iota(jnp.int32, (128, 128), 0)
    big_lane = lax.broadcasted_iota(jnp.int32, (128, 128), 1)

    def split_m(p):
        def go():
            for n in (2 * p, 2 * p + 1):
                for g in range(GROUPS):
                    tile = mraw[g, :, pl.ds(128 * n, 128)]
                    mh[n, pl.ds(FACE * g, FACE)], ml[n, pl.ds(FACE * g, FACE)] = halves(tile)
        return go

    def turn_m(n):
        def go():
            same = (big_sub >> 6) == (big_lane >> 6)
            place = jnp.where(same & ((pairs[n : n + 1] >> 6) == (big_sub & 63)), 1.0, 0.0).astype(BF16)
            rows = dot_t(place, mh[n]) + dot_t(place, ml[n])
            for q in range(2):
                turned_m[q, pl.ds(128 * n, 128)] = rows[:, 128 * q : 128 * q + 128]
        return go

    equal = (
        lax.broadcasted_iota(jnp.int32, (256, 256), 0) == lax.broadcasted_iota(jnp.int32, (256, 256), 1)
    ).astype(F32).astype(BF16)

    def order_m(n):
        def go():
            slab = []
            for q in range(2):
                slab.append(jnp.concatenate([
                    turned_m[q, pl.ds(core * FACE + 2 * n + k, 32, stride=128)] for k in range(2) for core in range(2)
                ], axis=0))
            high, low = halves(jnp.concatenate(slab, axis=1))
            nh[n] = dot_t(equal, high).astype(BF16)
            nl[n] = dot_t(equal, low).astype(BF16)
        return go

    def split_k(d, r):
        def go():
            kh[d, pl.ds(128 * r, 128)], kl[d, pl.ds(128 * r, 128)] = halves(kraw[d, pl.ds(128 * r, 128)])
        return go

    def split_u(w2, d):
        def go():
            uh[d], ul[d] = halves(w2[d])
        return go

    def face_out(it, w):
        def go():
            for k, (src, target) in enumerate((
                (w.at[:, 7], (up, y)),
                (w.at[:, 0], (down, y)),
                (w.at[:, :, 7], (s, (y + 1) % GROUPS)),
                (w.at[:, :, 0], (s, (y + GROUPS - 1) % GROUPS)),
            )):
                pltpu.make_async_remote_copy(
                    src_ref=src, dst_ref=halo.at[it, k], send_sem=hsend.at[it], recv_sem=hrecv.at[it],
                    device_id=target, device_id_type=MESH,
                ).start()
        return go

    def face_in(it):
        def go():
            pltpu.make_async_copy(halo.at[it], halo.at[it], hrecv.at[it]).wait()
        return go

    low_i = jnp.where(s > 0, 1.0, 0.0).astype(F32)
    high_i = jnp.where(s < NX * NZ * NC - 1, 1.0, 0.0).astype(F32)
    low_j = jnp.where(y > 0, 1.0, 0.0).astype(F32)
    high_j = jnp.where(y < GROUPS - 1, 1.0, 0.0).astype(F32)
    weight = damping * coupling

    layer = lax.broadcasted_iota(jnp.int32, (32, EDGE, FIELDS), 1)

    def volume(w2, o2, d, r):
        def go():
            block = pl.ds(256 * r, 256)
            applied = dot3(kh[d, block], kl[d, block], uh[d], ul[d])
            here = w2[d, block].reshape(32, EDGE, FIELDS)
            term = here
            if d + 1 < DEPTH:
                term = here - pltpu.roll(w2[d + 1, block].reshape(32, EDGE, FIELDS), 7, 1)
            term = jnp.where(layer == EDGE - 1, term, 0.0)
            if d:
                above = here - pltpu.roll(w2[d - 1, block].reshape(32, EDGE, FIELDS), 1, 1)
                term = jnp.where(layer == 0, above, term)
            out = w2[d, block] + damping * (ld[d, block] - applied)
            o2[d, block] = out - weight * term.reshape(256, FIELDS)
        return go

    def faces(it, w, o, w2, o2, d):
        def go():
            o[d, 0] -= weight * (w[d, 0] - low_i * halo[it, 0, d])
            o[d, 7] -= weight * (w[d, 7] - high_i * halo[it, 1, d])
            o[d, :, 0] -= weight * (w[d, :, 0] - low_j * halo[it, 2, d])
            o[d, :, 7] -= weight * (w[d, :, 7] - high_j * halo[it, 3, d])
        return go

    x2 = xb.reshape(2, 2, 64 * FACE, 128)

    def boundary(it, spots):
        def go():
            left_h, left_l, right = [], [], []
            for dx, dz in spots:
                n = chip(-dx, -dz)
                left_h.append((mh if it else nh)[n])
                left_l.append((ml if it else nl)[n])
                rows = pl.ds(pl.multiple_of(128 * n, 128), 128)
                right.append(jnp.concatenate([x2[it, 0, rows], x2[it, 1, rows]], axis=1))
            xh, xl = halves(jnp.concatenate(right, axis=0))
            part[...] += dot3(jnp.concatenate(left_h, axis=1), jnp.concatenate(left_l, axis=1), xh, xl)
        return go

    def put_x(it, rows):
        for h in range(2):
            xb[it, h, s] = rows[:, 128 * h : 128 * h + 128]

    def gather(it, tasks, pops):
        tasks = list(tasks)
        xr = xb.at[it]

        def send(p, block, target):
            pltpu.make_async_remote_copy(
                src_ref=xr.at[:, block, PARTS[p]], dst_ref=xr.at[:, block, PARTS[p]],
                send_sem=gsend.at[it], recv_sem=grecv.at[it, p, block],
                device_id=(target, y), device_id_type=MESH,
            ).start()

        def wait(p, block):
            piece = xr.at[:, block, PARTS[p]]
            pltpu.make_async_copy(piece, piece, grecv.at[it, p, block]).wait()

        def share(block):
            pltpu.make_async_remote_copy(
                src_ref=xr.at[:, block], dst_ref=xr.at[:, block],
                send_sem=gsend.at[it], recv_sem=grecv.at[it, 0, block],
                device_id=(sibling, y), device_id_type=MESH,
            ).start()

        def shared(spots):
            def go():
                for dx, dz in spots:
                    block = at(-dx, -dz) + sgn
                    pltpu.make_async_copy(xr.at[:, block], xr.at[:, block], grecv.at[it, 0, block]).wait()
            return go

        def work(now, most):
            while tasks and tasks[0][0] <= now and most:
                tasks.pop(0)[1]()
                most -= 1

        for p, dx, dz in FIRST:
            send(p, s, at(dx, dz))
        share(s)
        part[...] = jnp.zeros_like(part)
        work(-1, pops)
        seen, fresh = {(0, 0): 2}, [(0, 0)]
        for now, (p, dx, dz, onward) in enumerate(ARRIVALS):
            block = at(-dx, -dz)
            wait(p, block)
            for tx, tz in onward:
                send(p, block, at(tx, tz))
            seen[dx, dz] = seen.get((dx, dz), 0) + 1
            if seen[dx, dz] == 2:
                share(block)
                fresh.append((dx, dz))
            if now >= START[it] and len(fresh) > LAG:
                early, fresh = fresh[:2], fresh[2:]
                tasks[:0] = [(0, shared(early)), (0, boundary(it, early))]
            work(now, pops)
        work(99, 99)
        shared(fresh)()
        for i in range(0, len(fresh), 4):
            boundary(it, fresh[i : i + 4])()

    def reduce(it, tasks):
        for i in (2, 1, 3):
            other = (y + i) % GROUPS
            pltpu.make_async_remote_copy(
                src_ref=part.at[pl.ds(pl.multiple_of(FACE * other, FACE), FACE)], dst_ref=rsbuf.at[it, i - 1],
                send_sem=rsend.at[it], recv_sem=rrecv.at[it],
                device_id=(s, other), device_id_type=MESH,
            ).start()
        for task in tasks:
            task()
        own = part[pl.ds(pl.multiple_of(FACE * y, FACE), FACE)]
        pltpu.make_async_copy(rsbuf.at[it], rsbuf.at[it], rrecv.at[it]).wait()
        total = own + rsbuf[it, 0] + rsbuf[it, 1] + rsbuf[it, 2]
        three = part.at[pl.ds(0, 3 * FACE)]
        pltpu.make_async_copy(three, three, rsend.at[it]).wait()
        return total

    lead.wait()
    put_x(0, exact(node_out, u2[0]))
    pl.semaphore_wait(barrier, NX * NC - 1 + NZ - 1 + GROUPS - 1 + 1)
    early = [rest.wait] + [copy.wait for copy in get_m] + [split_m(p) for p in range(16)] + [turn_m(n) for n in range(32)] + [order_m(n) for n in range(32)]
    later = [get_k.wait] + [split_u(u2, d) for d in range(3)]
    later += [split_k(0, r) for r in range(4)] + [get_l.wait] + [volume(u2, v2, 0, r) for r in range(2)]
    tasks = [(-1, task) for task in early[:13]] + [(0, task) for task in early[13:]]
    tasks[13:13] = [(3, face_out(0, u))]
    tasks += [(0, task) for task in later]
    tasks += [(36, face_in(0)), (36, faces(0, u, v, u2, v2, 0))]
    tasks += [(36, lambda: rows_out(1, exact(node_out, v2[0])))]
    for d in (1, 2):
        tasks += [(0, split_k(d, r)) for r in range(4)] + [(0, volume(u2, v2, d, r)) for r in range(2)]
        tasks += [(0, faces(0, u, v, u2, v2, d))]
    tasks += [(56, lambda: rows_turn(1))]
    gather(0, tasks, 4)
    traction = reduce(0, [])
    put_x(1, exact(slot_in, rows_in(1)) - damping * traction)
    tr[...] = traction

    def first_top():
        v2[0] -= damping * exact(node_in, rows_in(2))
        pltpu.make_async_copy(halo.at[0], halo.at[0], hsend.at[0]).wait()

    tasks = [(-1, lambda: rows_out(2, exact(slot_out, tr[...]))), (10, lambda: rows_turn(2))]
    tasks += [(22, first_top), (22, face_out(1, v))] + [(22, split_u(v2, d)) for d in range(3)]
    for d in (2, 1, 0):
        tasks += [(0, volume(v2, u2, d, r)) for r in range(2)]
    gather(1, tasks, 3)
    deep = pltpu.make_async_copy(u2.at[pl.ds(1, 2)], sol.at[pl.ds(1, 2)], osem.at[0])
    traction = reduce(1, [])
    tr[...] = traction
    rows_out(3, exact(slot_out, traction))
    put_tr = pltpu.make_async_copy(tr, trac, osem.at[1])
    put_tr.start()
    rows_turn(3)
    for task in [face_in(1)] + [faces(1, v, u, v2, u2, d) for d in (2, 1, 0)] + [deep.start]:
        task()
    u2[0] -= damping * exact(node_in, rows_in(3))
    last = pltpu.make_async_copy(u2.at[0], sol.at[0], osem.at[2])
    last.start()

    for it in range(2):
        most = xb.at[it, :, pl.ds(0, 63)]
        pltpu.make_async_copy(most, most, gsend.at[it]).wait()
    pltpu.make_async_copy(halo.at[1], halo.at[1], hsend.at[1]).wait()
    for k in (1, 2, 3):
        for phase in range(2):
            seven = abuf.at[k, :, pl.ds(0, 56)]
            pltpu.make_async_copy(seven, seven, asend.at[k, phase]).wait()
    deep.wait()
    put_tr.wait()
    last.wait()


def shards(stiffness, load, start, boundary_matrix, bem_node):
    anywhere = pl.BlockSpec(memory_space=pl.ANY)
    vmem = pl.BlockSpec(memory_space=pltpu.VMEM)
    dma = pltpu.SemaphoreType.DMA
    field = (DEPTH, EDGE, EDGE, EDGE, FIELDS)
    flat = (DEPTH, NODES, FIELDS)
    sol, trac = pl.pallas_call(
        kernel,
        out_shape=(
            jax.ShapeDtypeStruct(flat, F32),
            jax.ShapeDtypeStruct((FACE, FIELDS), F32),
        ),
        in_specs=[anywhere] * 4 + [vmem],
        out_specs=(anywhere, anywhere),
        scratch_shapes=[
            pltpu.VMEM(field, F32), pltpu.VMEM(field, F32), pltpu.VMEM(flat, F32),
            pltpu.VMEM(flat, BF16), pltpu.VMEM(flat, BF16),
            pltpu.VMEM((DEPTH, NODES, NODES), F32),
            pltpu.VMEM((DEPTH, NODES, NODES), BF16), pltpu.VMEM((DEPTH, NODES, NODES), BF16),
            pltpu.VMEM((GROUPS, FACE, COLS), F32),
            *[pltpu.VMEM((32, 256, 128), BF16)] * 4,
            pltpu.VMEM((2, COLS, 128), F32),
            pltpu.VMEM((2, 2, 64, FACE, 128), F32),
            pltpu.VMEM((256, FIELDS), F32),
            pltpu.VMEM((2, 3, FACE, FIELDS), F32),
            pltpu.VMEM((2, 4, DEPTH, EDGE, EDGE, FIELDS), F32),
            pltpu.VMEM((FACE, FIELDS), F32),
            *[pltpu.VMEM((4, 2, FACE, 128), F32)] * 4,
            dma((9,)), dma((2,)), dma((2, 2, 64)), dma((4, 2)), dma((4, 2)),
            dma((2,)), dma((2,)), dma((2,)), dma((2,)), dma((3,)),
        ],
        compiler_params=pltpu.CompilerParams(
            collective_id=0, has_side_effects=True, vmem_limit_bytes=58 * 2**20
        ),
        name="interface_iterations",
    )(stiffness[0], load[0], start[0], boundary_matrix, bem_node.reshape(32, 128))
    return sol[None], trac[None]


def solution(mesh):
    in_specs = (
        P(("surf", "col"), None, None, None),
        P(("surf", "col"), None, None, None),
        P(("surf", "col"), None, None, None),
        P("surf", None, "col"),
        P("col", None),
    )
    out_specs = (P(("surf", "col"), None, None, None), P("col", "surf", None))
    return jax.shard_map(shards, mesh=mesh, in_specs=in_specs, out_specs=out_specs, check_vma=False)
```
